512 devices in a mesh: wide: 128 (over x, z, core), narrow: 4 (over y).
Axes of the slice: x: 4, y: 4, z: 16, core: 2. Of those that a mesh axis runs over, the one named last changes fastest.
Arguments:
- distance: float32 [128, 2048, 512], P('wide', None, 'narrow'), may hold values from -1 to 1
- occupancy: int32 [128, 256, 64], P('wide', None, 'narrow'), may hold values 0 or 1
- material: int32 [128, 256, 64], P('wide', None, 'narrow'), may hold values from 0 to 15
- colours: float32 [3, 16], replicated, may hold values from 0.1 to 1
- absorb: float32 [16], replicated, may hold values from 0.5 to 4
- kernel_x: float32 [256, 256], replicated, may hold values from -0.1875 to 0.1875
- kernel_y: float32 [128, 128], replicated, may hold values from -0.25 to 0.25
Outputs:
- image: float32 [4, 2048, 512], P(None, 'wide', 'narrow')
The draws below stay inside these ranges and needn't reach their ends.
All inputs are finite; a program needn't handle non-finite values. No bound on the sum of `occupancy` on one device may be relied on, other than what follows from the above.
Results may differ from the reference program's by a relative error of at most 0.0003.
Values sent between devices are 32-bit elements; how exact they have to be, the bound alone decides.
No kernel may reach another device: no remote copies, remote signals or barrier semaphores. Data moves between devices by JAX's collectives and lax.ppermute only.
A program may use at most 64 MiB of HBM per device.

```python
import math
import jax
import jax.numpy as jnp
from jax import lax

IX = 2048
XB = 256
YB = 128
BX = 8
BY = 8
MATS = 16
NZ = 128
NY = 512


def set_ends(drawn, stream_key, least, high):
    longest = drawn.shape.index(max(drawn.shape))
    spots = []
    for shift in (0, 1):
        where = [jax.random.randint(jax.random.fold_in(stream_key, axis), (), 0, length) for axis, length in enumerate(drawn.shape)]
        where[longest] = (where[longest] + shift) % drawn.shape[longest]
        spots.append(tuple(where))
    return drawn.at[spots[0]].set(least).at[spots[1]].set(high)


def steps_of(own_key, shape, shards, smallest, largest):
    factor_of, own = 1.0, jax.random.fold_in(own_key, 6)
    for position, shards_of in shards:
        draws = jnp.exp(jax.random.uniform(jax.random.fold_in(own, position), (shards_of,), jnp.float32, smallest / len(shards), largest / len(shards)))
        factor_of = factor_of * jnp.repeat(draws, shape[position] // shards_of).reshape([-1 if axis == position else 1 for axis in range(len(shape))])
    return factor_of


def noise(key, shape, width, limit, kind=jnp.bfloat16):
    return jnp.clip(width * jax.random.normal(key, shape, jnp.float32), -limit, limit).astype(kind)


def setup_inputs(seed: int = 0) -> dict:
    arg_keys = jax.random.split(jax.random.key(seed), 8)
    return {
        "distance": jnp.clip(jax.random.uniform(arg_keys[0], (NZ, IX, NY), jnp.float32, -1.0, 1.0) * steps_of(arg_keys[0], (NZ, IX, NY), ((0, 128), (2, 4)), -0.4, 0.0), -1.0, 1.0),
        "occupancy": set_ends((jax.random.randint(arg_keys[1], (NZ, IX // BX, NY // BY), 0, 4) < 3).astype(jnp.int32), jax.random.fold_in(arg_keys[1], 1), 0, 1),
        "material": set_ends(jax.random.randint(arg_keys[2], (NZ, IX // BX, NY // BY), 0, MATS), jax.random.fold_in(arg_keys[2], 1), 0, MATS - 1).astype(jnp.int32),
        "colours": jnp.clip(jax.random.uniform(arg_keys[3], (3, MATS), jnp.float32, 0.1, 1.0), 0.1, 1.0),
        "absorb": jnp.clip(jnp.exp(jax.random.uniform(arg_keys[4], (MATS,), jnp.float32, math.log(0.5), math.log(4.0))), 0.5, 4.0),
        "kernel_x": noise(arg_keys[5], (XB, XB), (4 * XB) ** -0.5, 0.1875, jnp.float32),
        "kernel_y": noise(arg_keys[6], (YB, YB), (4 * YB) ** -0.5, 0.25, jnp.float32),
    }


def resample(fields, kernel_x, kernel_y):
    leading = fields.shape[:-2]
    col_count = fields.shape[-2]
    row_count = fields.shape[-1]
    block_x = kernel_x.shape[0]
    block_y = kernel_y.shape[0]
    blocked = fields.reshape(leading + (col_count // block_x, block_x, row_count))
    blended = 0.5 * blocked + jnp.einsum('...bir,ij->...bjr', blocked, kernel_x, precision=lax.Precision.HIGHEST)
    blended = blended.reshape(leading + (col_count, row_count // block_y, block_y))
    blended = 0.5 * blended + jnp.einsum('...xci,ij->...xcj', blended, kernel_y, precision=lax.Precision.HIGHEST)
    return blended.reshape(fields.shape)

def expand(values, col_count, row_count):
    shape = values.shape
    brick_rows = shape[-1]
    brick_cols = shape[-2]
    row_ids = jnp.arange(row_count, dtype=jnp.int32) // (row_count // brick_rows)
    spread = (row_ids[None, :] == jnp.arange(brick_rows, dtype=jnp.int32)[:, None]).astype(jnp.float32)
    wider = jnp.einsum('...y,yr->...r', values, spread, precision=lax.Precision.HIGHEST)
    grown = jnp.broadcast_to(wider[..., :, None, :], shape[:-2] + (brick_cols, col_count // brick_cols, row_count))
    return grown.reshape(shape[:-2] + (col_count, row_count))

def brick_table(material, occupancy, colours, absorb):
    lookup = jnp.concatenate([colours, absorb[None, :]], axis=0)
    labels = jnp.arange(colours.shape[1], dtype=jnp.int32)
    selector = (material[None] == labels.reshape((-1,) + (1,) * material.ndim)).astype(jnp.float32)
    bricks = jnp.tensordot(lookup, selector, axes=((1,), (0,)), precision=lax.Precision.HIGHEST)
    return jnp.concatenate([bricks, occupancy.astype(jnp.float32)[None]], axis=0)

def shade(blended, brick_values, mask, step_length):
    dist_field = blended[0]
    density = jnp.exp(-2.0 * dist_field * dist_field)
    norm_sq = jnp.maximum(blended[1] * blended[1] + blended[2] * blended[2] + blended[3] * blended[3], 0.1)
    facing = 0.25 + 0.75 * jnp.abs(blended[3]) * lax.rsqrt(norm_sq)
    opacity = mask * (1.0 - jnp.exp(-brick_values[3] * density * step_length))
    colour = brick_values[:3] * (facing * opacity)[None]
    return (colour, opacity)

def reference(distance, occupancy, material, colours, absorb, kernel_x, kernel_y):
    depth_total, col_count, row_count = distance.shape
    step_length = 4.0 / NZ

    def one_slice(carry, depth_index):
        accumulated, transmit = carry
        current = lax.dynamic_index_in_dim(distance, depth_index, 0, keepdims=False)
        below = lax.dynamic_index_in_dim(distance, jnp.maximum(depth_index - 1, 0).astype(jnp.int32), 0, keepdims=False)
        below = below * (depth_index > 0).astype(jnp.float32)
        above = lax.dynamic_index_in_dim(distance, jnp.minimum(depth_index + 1, depth_total - 1).astype(jnp.int32), 0, keepdims=False)
        above = above * (depth_index < depth_total - 1).astype(jnp.float32)
        grad_z = 0.5 * (above - below)
        pad_cols = jnp.pad(current, ((1, 1), (0, 0)))
        grad_x = 0.5 * (pad_cols[2:] - pad_cols[:-2])
        pad_rows = jnp.pad(current, ((0, 0), (1, 1)))
        grad_y = 0.5 * (pad_rows[:, 2:] - pad_rows[:, :-2])
        blended = resample(jnp.stack([current, grad_x, grad_y, grad_z]), kernel_x, kernel_y)
        brick_mat = lax.dynamic_index_in_dim(material, depth_index, 0, keepdims=False)
        brick_occ = lax.dynamic_index_in_dim(occupancy, depth_index, 0, keepdims=False)
        table = brick_table(brick_mat, brick_occ, colours, absorb)
        brick_values = expand(table, col_count, row_count)
        colour, opacity = shade(blended, brick_values, brick_values[4], step_length)
        contrib = jnp.concatenate([colour, opacity[None]], axis=0)
        accumulated = accumulated + transmit[None] * contrib
        transmit = transmit * (1.0 - opacity)
        return ((accumulated, transmit), None)
    start = (jnp.zeros((4, col_count, row_count), jnp.float32), jnp.ones((col_count, row_count), jnp.float32))
    (accumulated, transmit), unused = lax.scan(one_slice, start, jnp.arange(depth_total, dtype=jnp.int32))
    return accumulated
```

```python
import jax
import jax.numpy as jnp
from jax import lax
from jax.experimental import pallas as pl
from jax.experimental.pallas import tpu as pltpu
from jax.sharding import Mesh, PartitionSpec as P

GROUP = ("zp", "core")
GROUPS = ("x", "zg")
WIDE = ("x", "zg", "zp", "core")
BLOCKS = 8
SLICES = 8
PIECES = 16
COLS = 256
ROWS = 128
PIECE = COLS // PIECES
FIELDS = 4
VMEM = pl.BlockSpec(memory_space=pltpu.VMEM)
SMEM = pl.BlockSpec(memory_space=pltpu.SMEM)


def halves(value):
    high = value.astype(jnp.bfloat16)
    low = (value - high.astype(jnp.float32)).astype(jnp.bfloat16)
    return high, low


def product(a, b, dims=((1,), (0,))):
    a_high, a_low = a
    b_high, b_low = b

    def one(p, q):
        return lax.dot_general(p, q, (dims, ((), ())), preferred_element_type=jnp.float32)

    return one(a_high, b_high) + (one(a_low, b_high) + one(a_high, b_low))


def ones_where(condition):
    return jnp.where(condition, 1.0, 0.0)


def iota(shape, dim):
    return lax.broadcasted_iota(jnp.int32, shape, dim)


def edges_kernel(cells, material, occupancy, first, last, base):
    ends = ones_where(
        (iota((8, ROWS), 0) == 0) & (iota((8, ROWS), 1) == 0)
        | (iota((8, ROWS), 0) == 1) & (iota((8, ROWS), 1) == ROWS - 1)
    )
    taken = lax.dot_general(
        ends,
        cells[0],
        (((1,), (1,)), ((), ())),
        precision=lax.Precision.HIGHEST,
        preferred_element_type=jnp.float32,
    )
    for part in range(2 * BLOCKS):
        first[part : part + 1] = taken[0:1, part * ROWS : (part + 1) * ROWS]
        last[part : part + 1] = taken[1:2, part * ROWS : (part + 1) * ROWS]
    brick_rows = material.shape[2]
    lane = iota((brick_rows, ROWS), 1)
    row = iota((brick_rows, ROWS), 0)
    kinds = material[0].astype(jnp.float32).reshape(BLOCKS, 4, 8, brick_rows)
    masks = occupancy[0].astype(jnp.float32).reshape(BLOCKS, 4, 8, brick_rows)
    packed = jnp.zeros((BLOCKS * 8, ROWS), jnp.float32)
    for part in range(4):
        at = 2 * brick_rows * part
        packed += jnp.dot(
            kinds[:, part].reshape(BLOCKS * 8, brick_rows),
            ones_where(lane == row + at),
            preferred_element_type=jnp.float32,
        )
        packed += jnp.dot(
            masks[:, part].reshape(BLOCKS * 8, brick_rows),
            ones_where(lane == row + (at + brick_rows)),
            preferred_element_type=jnp.float32,
        )
    none = jnp.zeros((1, ROWS), jnp.float32)
    for block in range(BLOCKS):
        left, right = block * COLS - 1, (block + 1) * COLS
        base[block, 0:1] = cells[0, left : left + 1] if block else none
        base[block, 1:2] = cells[0, right : right + 1] if block < BLOCKS - 1 else none
        base[block, 2:8] = jnp.zeros((6, ROWS), jnp.float32)
        base[block, 8:16] = packed[block * 8 : block * 8 + 8]


def block_kernel(
    cells, small, before, after, colours, absorb, kernel_x, kernel_y, image, fields, bricks, step
):
    eye_y = ones_where(iota((ROWS, ROWS), 0) == iota((ROWS, ROWS), 1))
    along_y = 0.5 * eye_y + kernel_y[...]
    none = jnp.zeros((1, ROWS), jnp.float32)
    slope_y = 0.5 * (
        jnp.concatenate([none, along_y[:-1]], axis=0) - jnp.concatenate([along_y[1:], none], axis=0)
    )
    both_y = halves(jnp.concatenate([along_y, slope_y], axis=1))
    only_y = halves(along_y)
    eye_x = ones_where(iota((COLS, COLS), 0) == iota((COLS, COLS), 1))
    along_x = halves((0.5 * eye_x + kernel_x[...]).T)
    beside = jnp.concatenate(
        [
            jnp.concatenate([small[s, 2 + 2 * side : 3 + 2 * side], small[s, 3 + 2 * side : 4 + 2 * side]], axis=1)
            for s in range(SLICES)
            for side in range(2)
        ],
        axis=0,
    )
    beside = halves(beside.T)
    corner = jnp.concatenate([-0.5 * along_y[0:1], 0.5 * along_y[-1:]], axis=0)
    column_ends = product(halves(small[:, 0:2, :].reshape(2 * SLICES, ROWS)), only_y)
    outer = product(
        halves(jnp.concatenate([before[...], after[...]], axis=0)), only_y
    )
    outer = jnp.concatenate([outer[:COLS], outer[COLS:]], axis=1)
    outer = product(along_x, halves(outer))
    fields[0] = outer[:, :ROWS]
    fields[SLICES + 1] = outer[:, ROWS:]
    for pair in range(SLICES // 2):
        parts = []
        for s in (2 * pair, 2 * pair + 1):
            rows = product(halves(cells[s]), both_y)
            value = rows[:, :ROWS]
            row = iota((2 * SLICES, ROWS), 0)
            wanted = jnp.where(row == 2 * s, corner[0:1], 0.0) + jnp.where(row == 2 * s + 1, corner[1:2], 0.0)
            slope = rows[:, ROWS:] + product(beside, halves(wanted))
            ahead = jnp.concatenate([value[1:], column_ends[2 * s + 1 : 2 * s + 2]], axis=0)
            behind = jnp.concatenate([column_ends[2 * s : 2 * s + 1], value[:-1]], axis=0)
            parts += [value, 0.5 * (ahead - behind), slope]
        mixed = product(along_x, halves(jnp.concatenate(parts, axis=1)))
        for i, s in enumerate((2 * pair, 2 * pair + 1)):
            at = 3 * i * ROWS
            fields[1 + s] = mixed[:, at : at + ROWS]
            u = mixed[:, at + ROWS : at + 2 * ROWS]
            v = mixed[:, at + 2 * ROWS : at + 3 * ROWS]
            fields[SLICES + 2 + s] = u * u + v * v
    codes = small[:, 8:16, :].reshape(SLICES * 8, ROWS)
    brick_rows = ROWS // 8
    masks = pltpu.roll(codes, ROWS - brick_rows, 1)
    values = [jnp.zeros_like(codes)] * FIELDS
    for label in range(colours.shape[1]):
        found = codes == float(label)
        for f in range(FIELDS):
            entry = colours[f, label] if f < 3 else absorb[label]
            values[f] = jnp.where(found, entry, values[f])
    values[3] = values[3] * masks * step
    values = jnp.concatenate(values, axis=0)
    source = iota((ROWS, 4 * ROWS), 0)
    target = iota((ROWS, 4 * ROWS), 1)
    spread = ones_where(source == (target // ROWS) * (2 * brick_rows) + (target % ROWS) // 8)
    spread = spread.astype(jnp.bfloat16)
    high, low = halves(values)
    least = (values - high.astype(jnp.float32) - low.astype(jnp.float32)).astype(jnp.bfloat16)
    grown = (
        jnp.dot(least, spread, preferred_element_type=jnp.float32)
        + jnp.dot(low, spread, preferred_element_type=jnp.float32)
        + jnp.dot(high, spread, preferred_element_type=jnp.float32)
    )
    for f in range(FIELDS):
        for s in range(SLICES):
            for part in range(4):
                bricks[f, s, 8 * part : 8 * part + 8] = grown[
                    (f * SLICES + s) * 8 : (f * SLICES + s) * 8 + 8, part * ROWS : (part + 1) * ROWS
                ]

    def shade(piece, _):
        for i in range(PIECE // 8):
            at = pl.ds(pl.multiple_of(piece * PIECE + 8 * i, 8), 8)
            brick = pl.ds(piece * (PIECE // 8) + i, 1)
            transmit = jnp.ones((8, ROWS), jnp.float32)
            total = [jnp.zeros((8, ROWS), jnp.float32)] * FIELDS
            for s in range(SLICES):
                d = fields[1 + s, at]
                w = 0.5 * (fields[2 + s, at] - fields[s, at])
                norm = jnp.maximum(fields[SLICES + 2 + s, at] + w * w, 0.1)
                facing = 0.25 + 0.75 * jnp.abs(w) * lax.rsqrt(norm)
                density = jnp.exp(-2.0 * d * d)
                opacity = 1.0 - jnp.exp(-bricks[3, s, brick] * density)
                weight = transmit * opacity
                shaded = weight * facing
                for f in range(3):
                    total[f] = total[f] + shaded * bricks[f, s, brick]
                total[3] = total[3] + weight
                transmit = transmit * (1.0 - opacity)
            for f in range(FIELDS):
                image[piece, f, 8 * i : 8 * i + 8] = total[f]
        return 0

    lax.fori_loop(0, PIECES, shade, 0)


def merge_kernel(parts, image):
    total = parts[0]
    for group in range(1, PIECES):
        total = total + (1.0 - total[3])[None] * parts[group]
    image[...] = total


def local(distance, occupancy, material, colours, absorb, kernel_x, kernel_y):
    slices, col_count, row_count = distance.shape
    wide = lax.axis_size(WIDE)
    narrow = lax.axis_size("narrow")
    groups = wide // SLICES
    f32 = jnp.float32
    cells = lax.all_to_all(distance.reshape(BLOCKS, COLS, ROWS), GROUP, 0, 0, tiled=True)
    first, last, base = pl.pallas_call(
        edges_kernel,
        out_shape=[
            jax.ShapeDtypeStruct((2 * BLOCKS, ROWS), f32),
            jax.ShapeDtypeStruct((2 * BLOCKS, ROWS), f32),
            jax.ShapeDtypeStruct((BLOCKS, 16, ROWS), f32),
        ],
        in_specs=[VMEM] * 3,
        out_specs=[VMEM] * 3,
        name="edges",
    )(distance, material, occupancy)
    up = lax.ppermute(last, "narrow", [(i, i + 1) for i in range(narrow - 1)])
    down = lax.ppermute(first, "narrow", [(i + 1, i) for i in range(narrow - 1)])
    small = jnp.concatenate(
        [base[:, :2], up.reshape(BLOCKS, 2, ROWS), down.reshape(BLOCKS, 2, ROWS), base[:, 6:]], axis=1
    )
    small = lax.all_to_all(small, GROUP, 0, 0, tiled=True)
    before = lax.ppermute(cells[-1], WIDE, [(i, i + SLICES) for i in range(wide - SLICES)])
    after = lax.ppermute(cells[0], WIDE, [(i + SLICES, i) for i in range(wide - SLICES)])
    step = 4.0 / (slices * wide)

    def block(*refs):
        block_kernel(*refs, step)

    pieces = pl.pallas_call(
        block,
        out_shape=jax.ShapeDtypeStruct((PIECES, FIELDS, PIECE, ROWS), f32),
        in_specs=[VMEM] * 4 + [SMEM] * 2 + [VMEM] * 2,
        out_specs=VMEM,
        scratch_shapes=[
            pltpu.VMEM((2 * SLICES + 2, COLS, ROWS), f32),
            pltpu.VMEM((FIELDS, SLICES, COLS // 8, ROWS), f32),
        ],
        compiler_params=pltpu.CompilerParams(vmem_limit_bytes=40 * 1024 * 1024),
        name="block",
    )(cells, small, before, after, colours, absorb, kernel_x, kernel_y)
    parts = lax.all_to_all(pieces, GROUPS, 0, 0, tiled=True)
    image = pl.pallas_call(
        merge_kernel,
        out_shape=jax.ShapeDtypeStruct((FIELDS, PIECE, ROWS), f32),
        in_specs=[VMEM],
        out_specs=VMEM,
        name="merge",
    )(parts)
    return lax.ppermute(
        image, WIDE, [(j * SLICES + i, i * groups + j) for j in range(groups) for i in range(SLICES)]
    )


def solution(mesh):
    wide, narrow = mesh.devices.shape
    split = Mesh(
        mesh.devices.reshape(4, wide // 32, 4, 2, narrow), ("x", "zg", "zp", "core", "narrow")
    )
    held = P(WIDE, None, "narrow")
    return jax.shard_map(
        local,
        mesh=split,
        in_specs=(held, held, held, P(), P(), P(), P()),
        out_specs=P(None, WIDE, "narrow"),
        check_vma=False,
    )
```

```python
import functools

import jax
import jax.numpy as jnp
from jax import lax
from jax.experimental import pallas as pl
from jax.experimental.pallas import tpu as pltpu
from jax.sharding import PartitionSpec as P

BLOCKS = 8
SLICES = 8
COLS = 256
ROWS = 128
PIECE = 16
NEAR = 8
PART = COLS // NEAR
FIELDS = 4
VMEM = pl.BlockSpec(memory_space=pltpu.VMEM)
SMEM = pl.BlockSpec(memory_space=pltpu.SMEM)


def halves(value):
    high = value.astype(jnp.bfloat16)
    low = (value - high.astype(jnp.float32)).astype(jnp.bfloat16)
    return high, low


def product(a, b, dims=((1,), (0,))):
    a_high, a_low = a
    b_high, b_low = b

    def one(p, q):
        return lax.dot_general(p, q, (dims, ((), ())), preferred_element_type=jnp.float32)

    return one(a_high, b_high) + (one(a_low, b_high) + one(a_high, b_low))


def ones_where(condition):
    return jnp.where(condition, 1.0, 0.0)


def iota(shape, dim):
    return lax.broadcasted_iota(jnp.int32, shape, dim)


def edges_kernel(cells, material, occupancy, first, last, base):
    ends = ones_where(
        (iota((8, ROWS), 0) == 0) & (iota((8, ROWS), 1) == 0)
        | (iota((8, ROWS), 0) == 1) & (iota((8, ROWS), 1) == ROWS - 1)
    )
    taken = lax.dot_general(
        ends,
        cells[0],
        (((1,), (1,)), ((), ())),
        precision=lax.Precision.HIGHEST,
        preferred_element_type=jnp.float32,
    )
    for block in range(BLOCKS):
        for part in range(2):
            at = (2 * block + part) * ROWS
            first[block, part : part + 1] = taken[0:1, at : at + ROWS]
            last[block, part : part + 1] = taken[1:2, at : at + ROWS]
    brick_rows = material.shape[2]
    lane = iota((brick_rows, ROWS), 1)
    row = iota((brick_rows, ROWS), 0)
    kinds = material[0].astype(jnp.float32).reshape(BLOCKS, 4, 8, brick_rows)
    masks = occupancy[0].astype(jnp.float32).reshape(BLOCKS, 4, 8, brick_rows)
    packed = jnp.zeros((BLOCKS * 8, ROWS), jnp.float32)
    for part in range(4):
        at = 2 * brick_rows * part
        packed += jnp.dot(
            kinds[:, part].reshape(BLOCKS * 8, brick_rows),
            ones_where(lane == row + at),
            preferred_element_type=jnp.float32,
        )
        packed += jnp.dot(
            masks[:, part].reshape(BLOCKS * 8, brick_rows),
            ones_where(lane == row + (at + brick_rows)),
            preferred_element_type=jnp.float32,
        )
    none = jnp.zeros((1, ROWS), jnp.float32)
    for block in range(BLOCKS):
        left, right = block * COLS - 1, (block + 1) * COLS
        base[block, 0:1] = cells[0, left : left + 1] if block else none
        base[block, 1:2] = cells[0, right : right + 1] if block < BLOCKS - 1 else none
        base[block, 2:8] = jnp.zeros((6, ROWS), jnp.float32)
        base[block, 8:16] = packed[block * 8 : block * 8 + 8]


def pack_kernel(base, up, down, small):
    small[...] = base[...]
    small[:, 2:4] = up[...]
    small[:, 4:6] = down[...]


def block_kernel(
    step, flip, cells, small, before, after, colours, absorb, kernel_x, kernel_y, image, fields, bricks
):
    place = [s ^ flip[0] for s in range(SLICES)]
    eye_y = ones_where(iota((ROWS, ROWS), 0) == iota((ROWS, ROWS), 1))
    along_y = 0.5 * eye_y + kernel_y[...]
    none = jnp.zeros((1, ROWS), jnp.float32)
    slope_y = 0.5 * (
        jnp.concatenate([none, along_y[:-1]], axis=0) - jnp.concatenate([along_y[1:], none], axis=0)
    )
    both_y = halves(jnp.concatenate([along_y, slope_y], axis=1))
    only_y = halves(along_y)
    eye_x = ones_where(iota((COLS, COLS), 0) == iota((COLS, COLS), 1))
    along_x = halves((0.5 * eye_x + kernel_x[...]).T)
    beside = jnp.concatenate(
        [
            jnp.concatenate([small[place[s], 2 + 2 * side : 3 + 2 * side], small[place[s], 3 + 2 * side : 4 + 2 * side]], axis=1)
            for s in range(SLICES)
            for side in range(2)
        ],
        axis=0,
    )
    beside = halves(beside.T)
    corner = jnp.concatenate([-0.5 * along_y[0:1], 0.5 * along_y[-1:]], axis=0)
    column_ends = jnp.concatenate([small[place[s], 0:2] for s in range(SLICES)], axis=0)
    column_ends = product(halves(column_ends), only_y)
    outer = product(
        halves(jnp.concatenate([before[...], after[...]], axis=0)), only_y
    )
    outer = jnp.concatenate([outer[:COLS], outer[COLS:]], axis=1)
    outer = product(along_x, halves(outer))
    fields[0] = outer[:, :ROWS]
    fields[SLICES + 1] = outer[:, ROWS:]
    for pair in range(SLICES // 2):
        parts = []
        for s in (2 * pair, 2 * pair + 1):
            rows = product(halves(cells[place[s]]), both_y)
            value = rows[:, :ROWS]
            row = iota((2 * SLICES, ROWS), 0)
            wanted = jnp.where(row == 2 * s, corner[0:1], 0.0) + jnp.where(row == 2 * s + 1, corner[1:2], 0.0)
            slope = rows[:, ROWS:] + product(beside, halves(wanted))
            ahead = jnp.concatenate([value[1:], column_ends[2 * s + 1 : 2 * s + 2]], axis=0)
            behind = jnp.concatenate([column_ends[2 * s : 2 * s + 1], value[:-1]], axis=0)
            parts += [value, 0.5 * (ahead - behind), slope]
        mixed = product(along_x, halves(jnp.concatenate(parts, axis=1)))
        for i, s in enumerate((2 * pair, 2 * pair + 1)):
            at = 3 * i * ROWS
            fields[1 + s] = mixed[:, at : at + ROWS]
            u = mixed[:, at + ROWS : at + 2 * ROWS]
            v = mixed[:, at + 2 * ROWS : at + 3 * ROWS]
            fields[SLICES + 2 + s] = u * u + v * v
    codes = small[:, 8:16, :].reshape(SLICES * 8, ROWS)
    brick_rows = ROWS // 8
    masks = pltpu.roll(codes, ROWS - brick_rows, 1)
    values = [jnp.zeros_like(codes)] * FIELDS
    for label in range(colours.shape[1]):
        found = codes == float(label)
        for f in range(FIELDS):
            entry = colours[f, label] if f < 3 else absorb[label]
            values[f] = jnp.where(found, entry, values[f])
    values[3] = values[3] * masks * step
    values = jnp.concatenate(values, axis=0)
    source = iota((ROWS, 4 * ROWS), 0)
    target = iota((ROWS, 4 * ROWS), 1)
    spread = ones_where(source == (target // ROWS) * (2 * brick_rows) + (target % ROWS) // 8)
    spread = spread.astype(jnp.bfloat16)
    high, low = halves(values)
    least = (values - high.astype(jnp.float32) - low.astype(jnp.float32)).astype(jnp.bfloat16)
    grown = (
        jnp.dot(least, spread, preferred_element_type=jnp.float32)
        + jnp.dot(low, spread, preferred_element_type=jnp.float32)
        + jnp.dot(high, spread, preferred_element_type=jnp.float32)
    )
    for f in range(FIELDS):
        for s in range(SLICES):
            for part in range(4):
                bricks[f, s, 8 * part : 8 * part + 8] = grown[
                    (f * SLICES + s) * 8 : (f * SLICES + s) * 8 + 8, part * ROWS : (part + 1) * ROWS
                ]

    def shade(piece, part):
        row = piece * (PART // 8) + part
        at = pl.ds(pl.multiple_of(row * 8, 8), 8)
        brick = pl.ds(row, 1)
        transmit = jnp.ones((8, ROWS), jnp.float32)
        total = [jnp.zeros((8, ROWS), jnp.float32)] * FIELDS
        for s in range(SLICES):
            d = fields[1 + s, at]
            w = 0.5 * (fields[2 + s, at] - fields[s, at])
            norm = jnp.maximum(fields[SLICES + 2 + s, at] + w * w, 0.1)
            facing = 0.25 + 0.75 * jnp.abs(w) * lax.rsqrt(norm)
            density = jnp.exp(-2.0 * d * d)
            opacity = 1.0 - jnp.exp(-bricks[3, place[s], brick] * density)
            weight = transmit * opacity
            shaded = weight * facing
            for f in range(3):
                total[f] = total[f] + shaded * bricks[f, place[s], brick]
            total[3] = total[3] + weight
            transmit = transmit * (1.0 - opacity)
        for f in range(FIELDS):
            image[piece, f, 8 * part : 8 * part + 8] = total[f]

    def shade_piece(piece, _):
        for part in range(PART // 8):
            shade(piece, part)
        return 0

    lax.fori_loop(0, NEAR, shade_piece, 0)


def over(nearer, farther):
    clear = 1.0 - nearer[3]
    return [nearer[f] + clear * farther[f] for f in range(FIELDS)]


def merge_near_kernel(half, parts, *out):
    for apart in range(2):
        chunk = half[0] ^ apart
        for i in range(PIECE // 8):
            at = pl.ds(pl.multiple_of(chunk * PIECE + 8 * i, 8), 8)
            total = [parts[0, f, at] for f in range(FIELDS)]
            for group in range(1, NEAR):
                total = over(total, [parts[group, f, at] for f in range(FIELDS)])
            for f in range(FIELDS):
                out[apart][f, 8 * i : 8 * i + 8] = total[f]


def merge_far_kernel(chunk, same, other, image):
    even = chunk[0] == 0
    for i in range(PIECE // 8):
        at = slice(8 * i, 8 * i + 8)
        pair = [(same[f, at], other[f, at]) for f in range(FIELDS)]
        total = over([jnp.where(even, a, b) for a, b in pair], [jnp.where(even, b, a) for a, b in pair])
        for f in range(FIELDS):
            image[f, at] = total[f]


def flip_of(group):
    return ((group >> 1) & 1) * (SLICES - 2)


def outer_blocks(distance, groups):
    chips = SLICES // 2
    me = lax.axis_index("wide")
    group, chip, core = me // SLICES, me % SLICES // 2, me % 2
    blocks = distance.reshape(chips, 2, COLS, ROWS)
    ends = [pair for k in range(groups) for pair in ((8 * k, 8 * k + 1), (8 * k + 7, 8 * k + 6))]
    shared = lax.ppermute(lax.dynamic_index_in_dim(blocks, 1 - core, 1, keepdims=False), "wide", ends)
    own = lax.dynamic_index_in_dim(blocks, core, 1, keepdims=False)
    first = chip == 0
    given = jnp.where(jnp.where(first, core == 0, core == 1), own, shared)
    before = after = jnp.zeros((COLS, ROWS), jnp.float32)
    for j in range(chips):
        back = chips - 1 - j
        pairs = []
        for k in range(groups - 1):
            for c in range(2):
                pairs.append((8 * k + 6 + c, 8 * (k + 1) + 2 * j + c))
                pairs.append((8 * (k + 1) + c, 8 * k + 2 * back + c))
        wanted = jnp.where(first, back ^ (flip_of(group - 1) // 2), j ^ (flip_of(group + 1) // 2))
        came = lax.ppermute(lax.dynamic_index_in_dim(given, wanted, 0, keepdims=False), "wide", pairs)
        before = jnp.where(chip == j, came, before)
        after = jnp.where(chip == back, came, after)
    return before, after


def local(distance, occupancy, material, colours, absorb, kernel_x, kernel_y):
    slices, col_count, row_count = distance.shape
    wide = lax.axis_size("wide")
    narrow = lax.axis_size("narrow")
    groups = wide // SLICES
    me = lax.axis_index("wide").astype(jnp.int32)
    group = me // SLICES
    flip = flip_of(group)
    holder = [[SLICES * k + (i ^ flip_of(k)) for i in range(SLICES)] for k in range(groups)]

    def one(*shape):
        return jax.ShapeDtypeStruct(shape, jnp.float32)

    cells = lax.all_to_all(
        distance.reshape(BLOCKS, COLS, ROWS), "wide", 0, 0, tiled=True, axis_index_groups=holder
    )
    first, last, base = pl.pallas_call(
        edges_kernel,
        out_shape=[one(BLOCKS, 2, ROWS), one(BLOCKS, 2, ROWS), one(BLOCKS, 16, ROWS)],
        in_specs=[VMEM] * 3,
        out_specs=[VMEM] * 3,
        name="edges",
    )(distance, material, occupancy)
    up = lax.ppermute(last, "narrow", [(i, i + 1) for i in range(narrow - 1)])
    down = lax.ppermute(first, "narrow", [(i + 1, i) for i in range(narrow - 1)])
    small = pl.pallas_call(
        pack_kernel,
        out_shape=one(BLOCKS, 16, ROWS),
        in_specs=[VMEM] * 3,
        out_specs=VMEM,
        name="pack",
    )(base, up, down)
    before, after = outer_blocks(distance, groups)
    cells, small, before, after = lax.optimization_barrier((cells, small, before, after))
    small = lax.all_to_all(small, "wide", 0, 0, tiled=True, axis_index_groups=holder)
    step = 4.0 / (slices * wide)
    pieces = pl.pallas_call(
        functools.partial(block_kernel, step),
        out_shape=one(NEAR, FIELDS, PART, ROWS),
        in_specs=[SMEM] + [VMEM] * 4 + [SMEM] * 2 + [VMEM] * 2,
        out_specs=VMEM,
        scratch_shapes=[
            pltpu.VMEM((2 * SLICES + 2, COLS, ROWS), jnp.float32),
            pltpu.VMEM((FIELDS, SLICES, COLS // 8, ROWS), jnp.float32),
        ],
        compiler_params=pltpu.CompilerParams(vmem_limit_bytes=40 * 1024 * 1024),
        name="block",
    )(flip.reshape(1), cells, small, before, after, colours, absorb, kernel_x, kernel_y)
    near = [[holder[k][i] for k in range(half, half + NEAR)] for i in range(SLICES) for half in range(0, groups, NEAR)]
    parts = lax.all_to_all(pieces, "wide", 0, 0, tiled=True, axis_index_groups=near)
    same, other = pl.pallas_call(
        merge_near_kernel,
        out_shape=[one(FIELDS, PIECE, ROWS)] * 2,
        in_specs=[SMEM, VMEM],
        out_specs=[VMEM] * 2,
        name="merge_near",
    )((group // NEAR).reshape(1), parts)
    came = []
    for apart, part in enumerate((same, other)):
        pairs = [
            (holder[k][i], groups * i + 2 * (k % NEAR) + (k // NEAR ^ apart))
            for k in range(groups)
            for i in range(SLICES)
        ]
        came.append(lax.ppermute(part, "wide", pairs))
    return pl.pallas_call(
        merge_far_kernel,
        out_shape=one(FIELDS, PIECE, ROWS),
        in_specs=[SMEM] + [VMEM] * 2,
        out_specs=VMEM,
        name="merge_far",
    )((me & 1).reshape(1), *came)


def solution(mesh):
    held = P("wide", None, "narrow")
    return jax.shard_map(
        local,
        mesh=mesh,
        in_specs=(held, held, held, P(), P(), P(), P()),
        out_specs=P(None, "wide", "narrow"),
        check_vma=False,
    )
```

```python
import functools

import jax
import jax.numpy as jnp
from jax import lax
from jax.experimental import pallas as pl
from jax.experimental.pallas import tpu as pltpu
from jax.sharding import PartitionSpec as P

BLOCKS = 8
SLICES = 8
COLS = 256
ROWS = 128
PIECE = 16
CHIPS = 8
MESSAGE = COLS + 16
FIELDS = 4
VMEM = pl.BlockSpec(memory_space=pltpu.VMEM)
SMEM = pl.BlockSpec(memory_space=pltpu.SMEM)
ANY = pl.BlockSpec(memory_space=pl.ANY)


def halves(value):
    high = value.astype(jnp.bfloat16)
    low = (value - high.astype(jnp.float32)).astype(jnp.bfloat16)
    return high, low


def product(a, b, dims=((1,), (0,))):
    a_high, a_low = a
    b_high, b_low = b

    def one(p, q):
        return lax.dot_general(p, q, (dims, ((), ())), preferred_element_type=jnp.float32)

    return one(a_high, b_high) + (one(a_low, b_high) + one(a_high, b_low))


def ones_where(condition):
    return jnp.where(condition, 1.0, 0.0)


def iota(shape, dim):
    return lax.broadcasted_iota(jnp.int32, shape, dim)


def thirds(value):
    high = value.astype(jnp.bfloat16)
    rest = value - high.astype(jnp.float32)
    middle = rest.astype(jnp.bfloat16)
    return high, middle, (rest - middle.astype(jnp.float32)).astype(jnp.bfloat16)


def message_kernel(cells, material, occupancy, message, first, last, sides, held, bricks, sems):
    load = pltpu.make_async_copy(cells.at[0], held, sems.at[0])
    load.start()
    copies = []
    brick_rows = material.shape[1]
    lane = iota((brick_rows, ROWS), 1)
    row = iota((brick_rows, ROWS), 0)
    kinds = material[0].astype(jnp.float32).T.reshape(BLOCKS, 4, 8, brick_rows)
    masks = occupancy[0].astype(jnp.float32).T.reshape(BLOCKS, 4, 8, brick_rows)
    packed = jnp.zeros((BLOCKS * 8, ROWS), jnp.float32)
    for part in range(4):
        at = 2 * brick_rows * part
        packed += jnp.dot(
            kinds[:, part].reshape(BLOCKS * 8, brick_rows),
            ones_where(lane == row + at),
            preferred_element_type=jnp.float32,
        )
        packed += jnp.dot(
            masks[:, part].reshape(BLOCKS * 8, brick_rows),
            ones_where(lane == row + (at + brick_rows)),
            preferred_element_type=jnp.float32,
        )
    bricks[...] = packed.reshape(BLOCKS, 8, ROWS)
    copies.append(pltpu.make_async_copy(bricks, message.at[:, COLS + 8 : MESSAGE], sems.at[1 + BLOCKS]))
    copies[-1].start()
    load.wait()
    for block in range(BLOCKS):
        copies.append(
            pltpu.make_async_copy(
                held.at[block * COLS : (block + 1) * COLS], message.at[block, :COLS], sems.at[1 + block]
            )
        )
        copies[-1].start()
    ends = ones_where(
        (iota((8, ROWS), 0) == 0) & (iota((8, ROWS), 1) == 0)
        | (iota((8, ROWS), 0) == 1) & (iota((8, ROWS), 1) == ROWS - 1)
    ).astype(jnp.bfloat16)
    for block in range(BLOCKS):
        left, right = block * COLS, (block + 1) * COLS
        taken = sum(
            lax.dot_general(ends, term, (((1,), (1,)), ((), ())), preferred_element_type=jnp.float32)
            for term in reversed(thirds(held[left:right]))
        )
        for part in range(2):
            at = part * ROWS
            first[block, part : part + 1] = taken[0:1, at : at + ROWS]
            last[block, part : part + 1] = taken[1:2, at : at + ROWS]
        none = jnp.zeros((1, ROWS), jnp.float32)
        sides[block, 0:1] = held[left - 1 : left] if block else none
        sides[block, 1:2] = held[right : right + 1] if block < BLOCKS - 1 else none
    for copy in copies:
        copy.wait()


def beside_kernel(_, sides, up, down, message, rows, sem):
    rows[:, 0:2] = sides[...]
    rows[:, 2:4] = up[...]
    rows[:, 4:6] = down[...]
    rows[:, 6:8] = jnp.zeros((BLOCKS, 2, ROWS), jnp.float32)
    copy = pltpu.make_async_copy(rows, message.at[:, COLS : COLS + 8], sem)
    copy.start()
    copy.wait()


def block_kernel(
    step, core, cells, before, after, colours, absorb, kernel_x, kernel_y, kept, given, fields, bricks
):
    eye_y = ones_where(iota((ROWS, ROWS), 0) == iota((ROWS, ROWS), 1))
    along_y = 0.5 * eye_y + kernel_y[...]
    none = jnp.zeros((1, ROWS), jnp.float32)
    slope_y = 0.5 * (
        jnp.concatenate([none, along_y[:-1]], axis=0) - jnp.concatenate([along_y[1:], none], axis=0)
    )
    both_y = halves(jnp.concatenate([along_y, slope_y], axis=1))
    only_y = halves(along_y)
    eye_x = ones_where(iota((COLS, COLS), 0) == iota((COLS, COLS), 1))
    along_x = halves((0.5 * eye_x + kernel_x[...]).T)
    beside = jnp.concatenate(
        [
            jnp.concatenate([cells[s, at : at + 1], cells[s, at + 1 : at + 2]], axis=1)
            for s in range(SLICES)
            for at in (COLS + 2, COLS + 4)
        ],
        axis=0,
    )
    beside = halves(beside.T)
    corner = jnp.concatenate([-0.5 * along_y[0:1], 0.5 * along_y[-1:]], axis=0)
    column_ends = jnp.concatenate([cells[s, COLS : COLS + 2] for s in range(SLICES)], axis=0)
    column_ends = product(halves(column_ends), only_y)
    outer = product(
        halves(jnp.concatenate([before[...], after[...]], axis=0)), only_y
    )
    outer = jnp.concatenate([outer[:COLS], outer[COLS:]], axis=1)
    outer = product(along_x, halves(outer))
    fields[0] = outer[:, :ROWS]
    fields[SLICES + 1] = outer[:, ROWS:]
    for pair in range(SLICES // 2):
        parts = []
        for s in (2 * pair, 2 * pair + 1):
            rows = product(halves(cells[s, :COLS]), both_y)
            value = rows[:, :ROWS]
            row = iota((2 * SLICES, ROWS), 0)
            wanted = jnp.where(row == 2 * s, corner[0:1], 0.0) + jnp.where(row == 2 * s + 1, corner[1:2], 0.0)
            slope = rows[:, ROWS:] + product(beside, halves(wanted))
            ahead = jnp.concatenate([value[1:], column_ends[2 * s + 1 : 2 * s + 2]], axis=0)
            behind = jnp.concatenate([column_ends[2 * s : 2 * s + 1], value[:-1]], axis=0)
            parts += [value, 0.5 * (ahead - behind), slope]
        mixed = product(along_x, halves(jnp.concatenate(parts, axis=1)))
        for i, s in enumerate((2 * pair, 2 * pair + 1)):
            at = 3 * i * ROWS
            fields[1 + s] = mixed[:, at : at + ROWS]
            u = mixed[:, at + ROWS : at + 2 * ROWS]
            v = mixed[:, at + 2 * ROWS : at + 3 * ROWS]
            fields[SLICES + 2 + s] = u * u + v * v
    codes = cells[:, COLS + 8 : MESSAGE, :].reshape(SLICES * 8, ROWS)
    brick_rows = ROWS // 8
    masks = pltpu.roll(codes, ROWS - brick_rows, 1)
    values = [jnp.zeros_like(codes)] * FIELDS
    for label in range(colours.shape[1]):
        found = codes == float(label)
        for f in range(FIELDS):
            entry = colours[f, label] if f < 3 else absorb[label]
            values[f] = jnp.where(found, entry, values[f])
    values[3] = values[3] * masks * step
    values = jnp.concatenate(values, axis=0)
    source = iota((ROWS, 4 * ROWS), 0)
    target = iota((ROWS, 4 * ROWS), 1)
    spread = ones_where(source == (target // ROWS) * (2 * brick_rows) + (target % ROWS) // 8)
    spread = spread.astype(jnp.bfloat16)
    high, low = halves(values)
    least = (values - high.astype(jnp.float32) - low.astype(jnp.float32)).astype(jnp.bfloat16)
    grown = (
        jnp.dot(least, spread, preferred_element_type=jnp.float32)
        + jnp.dot(low, spread, preferred_element_type=jnp.float32)
        + jnp.dot(high, spread, preferred_element_type=jnp.float32)
    )
    for f in range(FIELDS):
        for s in range(SLICES):
            for part in range(4):
                bricks[f, s, 8 * part : 8 * part + 8] = grown[
                    (f * SLICES + s) * 8 : (f * SLICES + s) * 8 + 8, part * ROWS : (part + 1) * ROWS
                ]

    def shade(image, piece, chunk, part):
        row = chunk * (PIECE // 8) + part
        at = pl.ds(pl.multiple_of(row * 8, 8), 8)
        brick = pl.ds(row, 1)
        transmit = jnp.ones((8, ROWS), jnp.float32)
        total = [jnp.zeros((8, ROWS), jnp.float32)] * FIELDS
        for s in range(SLICES):
            d = fields[1 + s, at]
            w = 0.5 * (fields[2 + s, at] - fields[s, at])
            norm = jnp.maximum(fields[SLICES + 2 + s, at] + w * w, 0.1)
            facing = 0.25 + 0.75 * jnp.abs(w) * lax.rsqrt(norm)
            density = jnp.exp(-2.0 * d * d)
            opacity = 1.0 - jnp.exp(-bricks[3, s, brick] * density)
            weight = transmit * opacity
            shaded = weight * facing
            for f in range(3):
                total[f] = total[f] + shaded * bricks[f, s, brick]
            total[3] = total[3] + weight
            transmit = transmit * (1.0 - opacity)
        for f in range(FIELDS):
            image[piece, f, 8 * part : 8 * part + 8] = total[f]

    def shade_chip(chip, _):
        for part in range(PIECE // 8):
            shade(given, chip, 2 * chip + (1 - core[0]), part)
            shade(kept, chip, 2 * chip + core[0], part)
        return 0

    lax.fori_loop(0, CHIPS, shade_chip, 0)


def over(nearer, farther):
    clear = 1.0 - nearer[3]
    return [nearer[f] + clear * farther[f] for f in range(FIELDS)]


def merge_z_kernel(core, parts, image):
    for block in range(4):
        for i in range(PIECE // 8):
            at = slice(8 * i, 8 * i + 8)
            total = None
            for group in range(4):
                chip = (4 * group + block) ^ (CHIPS * core[0])
                part = [parts[chip, f, at] for f in range(FIELDS)]
                total = over(total, part) if total else part
            for f in range(FIELDS):
                image[block, f, at] = total[f]


def merge_x_kernel(parts, image):
    for i in range(PIECE // 8):
        at = slice(8 * i, 8 * i + 8)
        total = [parts[0, f, at] for f in range(FIELDS)]
        for x in range(1, 4):
            total = over(total, [parts[x, f, at] for f in range(FIELDS)])
        for f in range(FIELDS):
            image[f, at] = total[f]


def outer_blocks(distance, groups):
    chips = SLICES // 2
    me = lax.axis_index("wide")
    chip, core = me % SLICES // 2, me % 2
    blocks = distance.reshape(chips, 2, COLS, ROWS)
    ends = [pair for k in range(groups) for pair in ((8 * k, 8 * k + 1), (8 * k + 7, 8 * k + 6))]
    shared = lax.ppermute(lax.dynamic_index_in_dim(blocks, 1 - core, 1, keepdims=False), "wide", ends)
    own = lax.dynamic_index_in_dim(blocks, core, 1, keepdims=False)
    first = chip == 0
    given = jnp.where(jnp.where(first, core == 0, core == 1), own, shared)
    before = after = jnp.zeros((COLS, ROWS), jnp.float32)
    for j in range(chips):
        back = chips - 1 - j
        pairs = []
        for k in range(groups - 1):
            for c in range(2):
                pairs.append((8 * k + 6 + c, 8 * (k + 1) + 2 * j + c))
                pairs.append((8 * (k + 1) + c, 8 * k + 2 * back + c))
        wanted = jnp.where(first, back, j)
        came = lax.ppermute(lax.dynamic_index_in_dim(given, wanted, 0, keepdims=False), "wide", pairs)
        before = jnp.where(chip == j, came, before)
        after = jnp.where(chip == back, came, after)
    return before, after


def local(distance, occupancy, material, colours, absorb, kernel_x, kernel_y):
    slices, col_count, row_count = distance.shape
    wide = lax.axis_size("wide")
    narrow = lax.axis_size("narrow")
    groups = wide // SLICES
    me = lax.axis_index("wide").astype(jnp.int32)
    core = (me & 1).reshape(1)
    members = [[SLICES * k + i for i in range(SLICES)] for k in range(groups)]

    def one(*shape):
        return jax.ShapeDtypeStruct(shape, jnp.float32)

    before, after = outer_blocks(distance, groups)
    message, first, last, sides = pl.pallas_call(
        message_kernel,
        out_shape=[one(BLOCKS, MESSAGE, ROWS)] + [one(BLOCKS, 2, ROWS)] * 3,
        in_specs=[ANY] + [VMEM] * 2,
        out_specs=[ANY] + [VMEM] * 3,
        scratch_shapes=[
            pltpu.VMEM((col_count, row_count), jnp.float32),
            pltpu.VMEM((BLOCKS, 8, ROWS), jnp.float32),
            pltpu.SemaphoreType.DMA((2 + BLOCKS,)),
        ],
        name="message",
    )(distance, jnp.swapaxes(material, 1, 2), jnp.swapaxes(occupancy, 1, 2))
    up = lax.ppermute(last, "narrow", [(i, i + 1) for i in range(narrow - 1)])
    down = lax.ppermute(first, "narrow", [(i + 1, i) for i in range(narrow - 1)])
    message = pl.pallas_call(
        beside_kernel,
        out_shape=one(BLOCKS, MESSAGE, ROWS),
        in_specs=[ANY] + [VMEM] * 3,
        out_specs=ANY,
        scratch_shapes=[pltpu.VMEM((BLOCKS, 8, ROWS), jnp.float32), pltpu.SemaphoreType.DMA],
        input_output_aliases={0: 0},
        name="beside",
    )(message, sides, up, down)
    cells = lax.all_to_all(message, "wide", 0, 0, tiled=True, axis_index_groups=members)
    step = 4.0 / (slices * wide)
    kept, given = pl.pallas_call(
        functools.partial(block_kernel, step),
        out_shape=[one(CHIPS, FIELDS, PIECE, ROWS)] * 2,
        in_specs=[SMEM] + [VMEM] * 3 + [SMEM] * 2 + [VMEM] * 2,
        out_specs=[VMEM] * 2,
        scratch_shapes=[
            pltpu.VMEM((2 * SLICES + 2, COLS, ROWS), jnp.float32),
            pltpu.VMEM((FIELDS, SLICES, COLS // 8, ROWS), jnp.float32),
        ],
        compiler_params=pltpu.CompilerParams(vmem_limit_bytes=40 * 1024 * 1024),
        name="block",
    )(core, cells, before, after, colours, absorb, kernel_x, kernel_y)
    taken = lax.ppermute(given, "wide", [(i, i ^ 1) for i in range(wide)])
    along_z = [
        [32 * x + 2 * ((z + CHIPS * c) % 16) + c for z in range(16)] for x in range(wide // 32) for c in range(2)
    ]
    parts = lax.all_to_all(
        jnp.concatenate([kept, taken], axis=0), "wide", 0, 0, tiled=True, axis_index_groups=along_z
    )
    parts = pl.pallas_call(
        merge_z_kernel,
        out_shape=one(4, FIELDS, PIECE, ROWS),
        in_specs=[SMEM, VMEM],
        out_specs=VMEM,
        name="merge_z",
    )(core, parts)
    along_x = [[32 * x + i for x in range(4)] for i in range(32)]
    parts = lax.all_to_all(parts, "wide", 0, 0, tiled=True, axis_index_groups=along_x)
    return pl.pallas_call(
        merge_x_kernel,
        out_shape=one(FIELDS, PIECE, ROWS),
        in_specs=[VMEM],
        out_specs=VMEM,
        name="merge_x",
    )(parts)


def solution(mesh):
    held = P("wide", None, "narrow")
    return jax.shard_map(
        local,
        mesh=mesh,
        in_specs=(held, held, held, P(), P(), P(), P()),
        out_specs=P(None, "wide", "narrow"),
        check_vma=False,
    )
```

```python
import functools

import jax
import jax.numpy as jnp
from jax import lax
from jax.experimental import pallas as pl
from jax.experimental.pallas import tpu as pltpu
from jax.sharding import PartitionSpec as P

BLOCKS = 8
SLICES = 8
COLS = 256
ROWS = 128
PIECE = 16
CHIPS = 8
MESSAGE = COLS + 16
FIELDS = 4
VMEM = pl.BlockSpec(memory_space=pltpu.VMEM)
SMEM = pl.BlockSpec(memory_space=pltpu.SMEM)
ANY = pl.BlockSpec(memory_space=pl.ANY)


def halves(value):
    high = value.astype(jnp.bfloat16)
    low = (value - high.astype(jnp.float32)).astype(jnp.bfloat16)
    return high, low


def product(a, b, dims=((1,), (0,))):
    a_high, a_low = a
    b_high, b_low = b

    def one(p, q):
        return lax.dot_general(p, q, (dims, ((), ())), preferred_element_type=jnp.float32)

    return one(a_high, b_high) + (one(a_low, b_high) + one(a_high, b_low))


def ones_where(condition):
    return jnp.where(condition, 1.0, 0.0)


def iota(shape, dim):
    return lax.broadcasted_iota(jnp.int32, shape, dim)


def thirds(value):
    high = value.astype(jnp.bfloat16)
    rest = value - high.astype(jnp.float32)
    middle = rest.astype(jnp.bfloat16)
    return high, middle, (rest - middle.astype(jnp.float32)).astype(jnp.bfloat16)


def message_kernel(cells, material, occupancy, message, held, sems):
    loads, stores = [], []
    for block in range(BLOCKS):
        loads.append(
            pltpu.make_async_copy(
                cells.at[0, block * COLS : (block + 1) * COLS], held.at[block, :COLS], sems.at[0, block]
            )
        )
        stores.append(pltpu.make_async_copy(held.at[block], message.at[block], sems.at[1, block]))
        loads[-1].start()
    brick_rows = material.shape[1]
    lane = iota((brick_rows, ROWS), 1)
    row = iota((brick_rows, ROWS), 0)
    kinds = material[0].astype(jnp.float32).T.reshape(BLOCKS, 4, 8, brick_rows)
    masks = occupancy[0].astype(jnp.float32).T.reshape(BLOCKS, 4, 8, brick_rows)
    packed = jnp.zeros((BLOCKS * 8, ROWS), jnp.float32)
    for part in range(4):
        at = 2 * brick_rows * part
        packed += jnp.dot(
            kinds[:, part].reshape(BLOCKS * 8, brick_rows),
            ones_where(lane == row + at),
            preferred_element_type=jnp.float32,
        )
        packed += jnp.dot(
            masks[:, part].reshape(BLOCKS * 8, brick_rows),
            ones_where(lane == row + (at + brick_rows)),
            preferred_element_type=jnp.float32,
        )
    ends = ones_where(
        (iota((8, ROWS), 0) == 0) & (iota((8, ROWS), 1) == 0)
        | (iota((8, ROWS), 0) == 1) & (iota((8, ROWS), 1) == ROWS - 1)
    ).astype(jnp.bfloat16)
    none = jnp.zeros((1, ROWS), jnp.float32)
    loads[0].wait()
    for block in range(BLOCKS):
        if block < BLOCKS - 1:
            loads[block + 1].wait()
        taken = sum(
            lax.dot_general(ends, term, (((1,), (1,)), ((), ())), preferred_element_type=jnp.float32)
            for term in reversed(thirds(held[block, :COLS]))
        )
        held[block, COLS : COLS + 1] = held[block - 1, COLS - 1 : COLS] if block else none
        held[block, COLS + 1 : COLS + 2] = held[block + 1, 0:1] if block < BLOCKS - 1 else none
        for end in range(2):
            for part in range(2):
                at = COLS + 2 + 2 * end + part
                held[block, at : at + 1] = taken[end : end + 1, part * ROWS : (part + 1) * ROWS]
        held[block, COLS + 6 : COLS + 8] = jnp.zeros((2, ROWS), jnp.float32)
        held[block, COLS + 8 : MESSAGE] = packed[block * 8 : block * 8 + 8]
        stores[block].start()
    for store in stores:
        store.wait()


def block_kernel(
    step, core, cells, up, down, before, after, colours, absorb, kernel_x, kernel_y, kept, given, fields, bricks
):
    eye_y = ones_where(iota((ROWS, ROWS), 0) == iota((ROWS, ROWS), 1))
    along_y = 0.5 * eye_y + kernel_y[...]
    none = jnp.zeros((1, ROWS), jnp.float32)
    slope_y = 0.5 * (
        jnp.concatenate([none, along_y[:-1]], axis=0) - jnp.concatenate([along_y[1:], none], axis=0)
    )
    both_y = halves(jnp.concatenate([along_y, slope_y], axis=1))
    only_y = halves(along_y)
    eye_x = ones_where(iota((COLS, COLS), 0) == iota((COLS, COLS), 1))
    along_x = halves((0.5 * eye_x + kernel_x[...]).T)
    beside = jnp.concatenate(
        [
            jnp.concatenate([rows[s, 0:1], rows[s, 1:2]], axis=1)
            for s in range(SLICES)
            for rows in (up, down)
        ],
        axis=0,
    )
    beside = halves(beside.T)
    corner = jnp.concatenate([-0.5 * along_y[0:1], 0.5 * along_y[-1:]], axis=0)
    column_ends = jnp.concatenate([cells[s, COLS : COLS + 2] for s in range(SLICES)], axis=0)
    column_ends = product(halves(column_ends), only_y)
    outer = product(
        halves(jnp.concatenate([before[...], after[...]], axis=0)), only_y
    )
    outer = jnp.concatenate([outer[:COLS], outer[COLS:]], axis=1)
    outer = product(along_x, halves(outer))
    fields[0] = outer[:, :ROWS]
    fields[SLICES + 1] = outer[:, ROWS:]
    for pair in range(SLICES // 2):
        parts = []
        for s in (2 * pair, 2 * pair + 1):
            rows = product(halves(cells[s, :COLS]), both_y)
            value = rows[:, :ROWS]
            row = iota((2 * SLICES, ROWS), 0)
            wanted = jnp.where(row == 2 * s, corner[0:1], 0.0) + jnp.where(row == 2 * s + 1, corner[1:2], 0.0)
            slope = rows[:, ROWS:] + product(beside, halves(wanted))
            ahead = jnp.concatenate([value[1:], column_ends[2 * s + 1 : 2 * s + 2]], axis=0)
            behind = jnp.concatenate([column_ends[2 * s : 2 * s + 1], value[:-1]], axis=0)
            parts += [value, 0.5 * (ahead - behind), slope]
        mixed = product(along_x, halves(jnp.concatenate(parts, axis=1)))
        for i, s in enumerate((2 * pair, 2 * pair + 1)):
            at = 3 * i * ROWS
            fields[1 + s] = mixed[:, at : at + ROWS]
            u = mixed[:, at + ROWS : at + 2 * ROWS]
            v = mixed[:, at + 2 * ROWS : at + 3 * ROWS]
            fields[SLICES + 2 + s] = u * u + v * v
    codes = cells[:, COLS + 8 : MESSAGE, :].reshape(SLICES * 8, ROWS)
    brick_rows = ROWS // 8
    masks = pltpu.roll(codes, ROWS - brick_rows, 1)
    values = [jnp.zeros_like(codes)] * FIELDS
    for label in range(colours.shape[1]):
        found = codes == float(label)
        for f in range(FIELDS):
            entry = colours[f, label] if f < 3 else absorb[label]
            values[f] = jnp.where(found, entry, values[f])
    values[3] = values[3] * masks * step
    values = jnp.concatenate(values, axis=0)
    source = iota((ROWS, 4 * ROWS), 0)
    target = iota((ROWS, 4 * ROWS), 1)
    spread = ones_where(source == (target // ROWS) * (2 * brick_rows) + (target % ROWS) // 8)
    spread = spread.astype(jnp.bfloat16)
    high, low = halves(values)
    least = (values - high.astype(jnp.float32) - low.astype(jnp.float32)).astype(jnp.bfloat16)
    grown = (
        jnp.dot(least, spread, preferred_element_type=jnp.float32)
        + jnp.dot(low, spread, preferred_element_type=jnp.float32)
        + jnp.dot(high, spread, preferred_element_type=jnp.float32)
    )
    for f in range(FIELDS):
        for s in range(SLICES):
            for part in range(4):
                bricks[f, s, 8 * part : 8 * part + 8] = grown[
                    (f * SLICES + s) * 8 : (f * SLICES + s) * 8 + 8, part * ROWS : (part + 1) * ROWS
                ]

    def shade(image, piece, chunk, part):
        row = chunk * (PIECE // 8) + part
        at = pl.ds(pl.multiple_of(row * 8, 8), 8)
        brick = pl.ds(row, 1)
        transmit = jnp.ones((8, ROWS), jnp.float32)
        total = [jnp.zeros((8, ROWS), jnp.float32)] * FIELDS
        for s in range(SLICES):
            d = fields[1 + s, at]
            w = 0.5 * (fields[2 + s, at] - fields[s, at])
            norm = jnp.maximum(fields[SLICES + 2 + s, at] + w * w, 0.1)
            facing = 0.25 + 0.75 * jnp.abs(w) * lax.rsqrt(norm)
            density = jnp.exp(-2.0 * d * d)
            opacity = 1.0 - jnp.exp(-bricks[3, s, brick] * density)
            weight = transmit * opacity
            shaded = weight * facing
            for f in range(3):
                total[f] = total[f] + shaded * bricks[f, s, brick]
            total[3] = total[3] + weight
            transmit = transmit * (1.0 - opacity)
        for f in range(FIELDS):
            image[piece, f, 8 * part : 8 * part + 8] = total[f]

    def shade_chip(chip, _):
        for part in range(PIECE // 8):
            shade(given, chip, 2 * chip + (1 - core[0]), part)
            shade(kept, chip, 2 * chip + core[0], part)
        return 0

    lax.fori_loop(0, CHIPS, shade_chip, 0)


def over(nearer, farther):
    return nearer + (1.0 - nearer[..., 3:4, :, :]) * farther


def outer_blocks(distance, groups):
    chips = SLICES // 2
    me = lax.axis_index("wide")
    chip, core = me % SLICES // 2, me % 2
    blocks = distance.reshape(chips, 2, COLS, ROWS)
    ends = [pair for k in range(groups) for pair in ((8 * k, 8 * k + 1), (8 * k + 7, 8 * k + 6))]
    shared = lax.ppermute(lax.dynamic_index_in_dim(blocks, 1 - core, 1, keepdims=False), "wide", ends)
    own = lax.dynamic_index_in_dim(blocks, core, 1, keepdims=False)
    first = chip == 0
    given = jnp.where(jnp.where(first, core == 0, core == 1), own, shared)
    before = after = jnp.zeros((COLS, ROWS), jnp.float32)
    for j in range(chips):
        back = chips - 1 - j
        pairs = []
        for k in range(groups - 1):
            for c in range(2):
                pairs.append((8 * k + 6 + c, 8 * (k + 1) + 2 * j + c))
                pairs.append((8 * (k + 1) + c, 8 * k + 2 * back + c))
        wanted = jnp.where(first, back, j)
        came = lax.ppermute(lax.dynamic_index_in_dim(given, wanted, 0, keepdims=False), "wide", pairs)
        before = jnp.where(chip == j, came, before)
        after = jnp.where(chip == back, came, after)
    return before, after


def local(distance, occupancy, material, colours, absorb, kernel_x, kernel_y):
    slices, col_count, row_count = distance.shape
    wide = lax.axis_size("wide")
    narrow = lax.axis_size("narrow")
    groups = wide // SLICES
    me = lax.axis_index("wide").astype(jnp.int32)
    core = (me & 1).reshape(1)
    members = [[SLICES * k + i for i in range(SLICES)] for k in range(groups)]

    def one(*shape):
        return jax.ShapeDtypeStruct(shape, jnp.float32)

    before, after = outer_blocks(distance, groups)
    message = pl.pallas_call(
        message_kernel,
        out_shape=one(BLOCKS, MESSAGE, ROWS),
        in_specs=[ANY] + [VMEM] * 2,
        out_specs=ANY,
        scratch_shapes=[pltpu.VMEM((BLOCKS, MESSAGE, ROWS), jnp.float32), pltpu.SemaphoreType.DMA((2, BLOCKS))],
        name="message",
    )(distance, jnp.swapaxes(material, 1, 2), jnp.swapaxes(occupancy, 1, 2))
    cells = lax.all_to_all(message, "wide", 0, 0, tiled=True, axis_index_groups=members)
    up = lax.ppermute(cells[:, COLS + 4 : COLS + 6], "narrow", [(i, i + 1) for i in range(narrow - 1)])
    down = lax.ppermute(cells[:, COLS + 2 : COLS + 4], "narrow", [(i + 1, i) for i in range(narrow - 1)])
    step = 4.0 / (slices * wide)
    kept, given = pl.pallas_call(
        functools.partial(block_kernel, step),
        out_shape=[one(CHIPS, FIELDS, PIECE, ROWS)] * 2,
        in_specs=[SMEM] + [VMEM] * 5 + [SMEM] * 2 + [VMEM] * 2,
        out_specs=[VMEM] * 2,
        scratch_shapes=[
            pltpu.VMEM((2 * SLICES + 2, COLS, ROWS), jnp.float32),
            pltpu.VMEM((FIELDS, SLICES, COLS // 8, ROWS), jnp.float32),
        ],
        compiler_params=pltpu.CompilerParams(vmem_limit_bytes=24 * 1024 * 1024),
        name="block",
    )(core, cells, up, down, before, after, colours, absorb, kernel_x, kernel_y)
    taken = lax.ppermute(given, "wide", [(i, i ^ 1) for i in range(wide)])
    along_z = [
        [32 * x + 2 * ((z + CHIPS * c) % 16) + c for z in range(16)] for x in range(wide // 32) for c in range(2)
    ]
    parts = lax.all_to_all(
        jnp.concatenate([kept, taken], axis=0), "wide", 0, 0, tiled=True, axis_index_groups=along_z
    )
    parts = parts.reshape(2, 2, 4, FIELDS, PIECE, ROWS)
    halves_z = [over(parts[h, 0], parts[h, 1]) for h in range(2)]
    front = core[0] == 0
    parts = over(jnp.where(front, halves_z[0], halves_z[1]), jnp.where(front, halves_z[1], halves_z[0]))
    along_x = [[32 * x + i for x in range(4)] for i in range(32)]
    parts = lax.all_to_all(parts, "wide", 0, 0, tiled=True, axis_index_groups=along_x)
    return over(over(parts[0], parts[1]), over(parts[2], parts[3]))


def solution(mesh):
    held = P("wide", None, "narrow")
    return jax.shard_map(
        local,
        mesh=mesh,
        in_specs=(held, held, held, P(), P(), P(), P()),
        out_specs=P(None, "wide", "narrow"),
        check_vma=False,
    )
```

```python
import functools

import jax
import jax.numpy as jnp
from jax import lax
from jax.experimental import pallas as pl
from jax.experimental.pallas import tpu as pltpu
from jax.sharding import PartitionSpec as P

BLOCKS = 8
SLICES = 8
COLS = 256
ROWS = 128
PIECE = 16
CHIPS = 8
MESSAGE = COLS + 16
FIELDS = 4
VMEM = pl.BlockSpec(memory_space=pltpu.VMEM)
SMEM = pl.BlockSpec(memory_space=pltpu.SMEM)
ANY = pl.BlockSpec(memory_space=pl.ANY)


def halves(value):
    high = value.astype(jnp.bfloat16)
    low = (value - high.astype(jnp.float32)).astype(jnp.bfloat16)
    return high, low


def product(a, b, dims=((1,), (0,))):
    a_high, a_low = a
    b_high, b_low = b

    def one(p, q):
        return lax.dot_general(p, q, (dims, ((), ())), preferred_element_type=jnp.float32)

    return one(a_high, b_high) + (one(a_low, b_high) + one(a_high, b_low))


def joined(a, b):
    a_high, a_low = a
    b_high, b_low = b
    return jnp.dot(
        jnp.concatenate([a_high, a_low, a_high], axis=1),
        jnp.concatenate([b_high, b_high, b_low], axis=0),
        preferred_element_type=jnp.float32,
    )


def ones_where(condition):
    return jnp.where(condition, 1.0, 0.0)


def iota(shape, dim):
    return lax.broadcasted_iota(jnp.int32, shape, dim)


def message_kernel(cells, material, occupancy, message, held, tail, sems):
    loads, stores = [], []
    for block in range(BLOCKS):
        part = held.at[block * COLS : (block + 1) * COLS]
        loads.append(pltpu.make_async_copy(cells.at[0, block * COLS : (block + 1) * COLS], part, sems.at[0, block]))
        stores.append(pltpu.make_async_copy(part, message.at[block, :COLS], sems.at[1, block]))
        loads[-1].start()
    brick_rows = material.shape[1]
    lane = iota((brick_rows, ROWS), 1)
    row = iota((brick_rows, ROWS), 0)
    kinds = material[0].astype(jnp.float32).T.reshape(BLOCKS, 4, 8, brick_rows)
    masks = occupancy[0].astype(jnp.float32).T.reshape(BLOCKS, 4, 8, brick_rows)
    packed = jnp.zeros((BLOCKS * 8, ROWS), jnp.float32)
    for part in range(4):
        at = 2 * brick_rows * part
        packed += jnp.dot(
            kinds[:, part].reshape(BLOCKS * 8, brick_rows),
            ones_where(lane == row + at),
            preferred_element_type=jnp.float32,
        )
        packed += jnp.dot(
            masks[:, part].reshape(BLOCKS * 8, brick_rows),
            ones_where(lane == row + (at + brick_rows)),
            preferred_element_type=jnp.float32,
        )
    ends = jnp.zeros((COLS, ROWS), jnp.float32)
    lane = iota((COLS, ROWS), 1)
    for block in range(BLOCKS):
        loads[block].wait()
        stores[block].start()
        turned = pltpu.roll(held[block * COLS : (block + 1) * COLS], 2 * block + 1, 1)
        ends = jnp.where(lane // 2 == block, turned, ends)
    ends = ends.T
    none = jnp.zeros((1, ROWS), jnp.float32)
    for block in range(BLOCKS):
        left, right = block * COLS, (block + 1) * COLS
        tail[block, 0:1] = held[left - 1 : left] if block else none
        tail[block, 1:2] = held[right : right + 1] if block < BLOCKS - 1 else none
        for end in range(2):
            row = 2 * block + 1 - end
            for part in range(2):
                at = 2 + 2 * end + part
                tail[block, at : at + 1] = ends[row : row + 1, part * ROWS : (part + 1) * ROWS]
        tail[block, 6:8] = jnp.zeros((2, ROWS), jnp.float32)
        tail[block, 8:16] = packed[block * 8 : block * 8 + 8]
    stores.append(pltpu.make_async_copy(tail, message.at[:, COLS:MESSAGE], sems.at[0, 0]))
    stores[-1].start()
    for store in stores:
        store.wait()


def weights(kernel):
    size = kernel.shape[0]
    return 0.5 * ones_where(iota((size, size), 0) == iota((size, size), 1)) + kernel[...]


def fields_kernel(
    step, cells, before, after, colours, absorb, kernel_x, kernel_y, distances, slopes_x, slopes_y, bricks
):
    along_x = halves(weights(kernel_x).T)
    along_y = weights(kernel_y)
    none = jnp.zeros((1, ROWS), jnp.float32)
    slope_y = 0.5 * (
        jnp.concatenate([none, along_y[:-1]], axis=0) - jnp.concatenate([along_y[1:], none], axis=0)
    )
    only_y = halves(along_y)
    both_y = halves(jnp.concatenate([along_y, slope_y], axis=1))
    column_ends = jnp.concatenate([cells[s, COLS : COLS + 2] for s in range(SLICES)], axis=0)
    column_ends = product(halves(column_ends), only_y)
    outer = joined(halves(jnp.concatenate([before[...], after[...]], axis=0)), only_y)
    outer = jnp.concatenate([outer[:COLS], outer[COLS:]], axis=1)
    outer = joined(along_x, halves(outer))
    distances[0] = outer[:, :ROWS]
    distances[SLICES + 1] = outer[:, ROWS:]
    for pair in range(SLICES // 2):
        parts = []
        for s in (2 * pair, 2 * pair + 1):
            rows = joined(halves(cells[s, :COLS]), both_y)
            value = rows[:, :ROWS]
            ahead = jnp.concatenate([value[1:], column_ends[2 * s + 1 : 2 * s + 2]], axis=0)
            behind = jnp.concatenate([column_ends[2 * s : 2 * s + 1], value[:-1]], axis=0)
            parts += [value, 0.5 * (ahead - behind), rows[:, ROWS:]]
        mixed = joined(along_x, halves(jnp.concatenate(parts, axis=1)))
        for i, s in enumerate((2 * pair, 2 * pair + 1)):
            at = 3 * i * ROWS
            distances[1 + s] = mixed[:, at : at + ROWS]
            slopes_x[s] = mixed[:, at + ROWS : at + 2 * ROWS]
            slopes_y[s] = mixed[:, at + 2 * ROWS : at + 3 * ROWS]
    codes = cells[:, COLS + 8 : MESSAGE, :].reshape(SLICES * 8, ROWS)
    brick_rows = ROWS // 8
    masks = pltpu.roll(codes, ROWS - brick_rows, 1)
    values = [jnp.zeros_like(codes)] * FIELDS
    for label in range(colours.shape[1]):
        found = codes == float(label)
        for f in range(FIELDS):
            entry = colours[f, label] if f < 3 else absorb[label]
            values[f] = jnp.where(found, entry, values[f])
    values[3] = values[3] * masks * step
    values = jnp.concatenate(values, axis=0)
    source = iota((ROWS, 4 * ROWS), 0)
    target = iota((ROWS, 4 * ROWS), 1)
    spread = ones_where(source == (target // ROWS) * (2 * brick_rows) + (target % ROWS) // 8)
    spread = spread.astype(jnp.bfloat16)
    high, low = halves(values)
    least = (values - high.astype(jnp.float32) - low.astype(jnp.float32)).astype(jnp.bfloat16)
    grown = (
        jnp.dot(least, spread, preferred_element_type=jnp.float32)
        + jnp.dot(low, spread, preferred_element_type=jnp.float32)
        + jnp.dot(high, spread, preferred_element_type=jnp.float32)
    )
    for f in range(FIELDS):
        for s in range(SLICES):
            for part in range(4):
                bricks[f, s, 8 * part : 8 * part + 8] = grown[
                    (f * SLICES + s) * 8 : (f * SLICES + s) * 8 + 8, part * ROWS : (part + 1) * ROWS
                ]


def shade_kernel(core, up, down, kernel_x, kernel_y, distances, slopes_x, slopes_y, bricks, kept, given, edges):
    beside = jnp.concatenate(
        [
            jnp.concatenate([rows[s, 0:1], rows[s, 1:2]], axis=1)
            for s in range(SLICES)
            for rows in (up, down)
        ],
        axis=0,
    )
    beside = halves(product(halves(beside), halves(weights(kernel_x))).T)
    along_y = weights(kernel_y)
    row = iota((2 * SLICES, ROWS), 0)
    for s in range(SLICES):
        wanted = jnp.where(row == 2 * s, -0.5 * along_y[0:1], 0.0) + jnp.where(
            row == 2 * s + 1, 0.5 * along_y[ROWS - 1 : ROWS], 0.0
        )
        edges[s] = product(beside, halves(wanted))

    def shade(image, piece, chunk, part):
        row = chunk * (PIECE // 8) + part
        at = pl.ds(pl.multiple_of(row * 8, 8), 8)
        brick = pl.ds(row, 1)
        transmit = jnp.ones((8, ROWS), jnp.float32)
        total = [jnp.zeros((8, ROWS), jnp.float32)] * FIELDS
        for s in range(SLICES):
            d = distances[1 + s, at]
            u = slopes_x[s, at]
            v = slopes_y[s, at] + edges[s, at]
            w = 0.5 * (distances[2 + s, at] - distances[s, at])
            norm = jnp.maximum(u * u + v * v + w * w, 0.1)
            facing = 0.25 + 0.75 * jnp.abs(w) * lax.rsqrt(norm)
            density = jnp.exp(-2.0 * d * d)
            opacity = 1.0 - jnp.exp(-bricks[3, s, brick] * density)
            weight = transmit * opacity
            shaded = weight * facing
            for f in range(3):
                total[f] = total[f] + shaded * bricks[f, s, brick]
            total[3] = total[3] + weight
            transmit = transmit * (1.0 - opacity)
        for f in range(FIELDS):
            image[piece, f, 8 * part : 8 * part + 8] = total[f]

    def shade_chip(chip, _):
        for part in range(PIECE // 8):
            shade(given, chip, 2 * chip + (1 - core[0]), part)
            shade(kept, chip, 2 * chip + core[0], part)
        return 0

    lax.fori_loop(0, CHIPS, shade_chip, 0)


def over(nearer, farther):
    return nearer + (1.0 - nearer[..., 3:4, :, :]) * farther


def outer_blocks(distance, groups):
    chips = SLICES // 2
    me = lax.axis_index("wide")
    chip, core = me % SLICES // 2, me % 2
    blocks = distance.reshape(chips, 2, COLS, ROWS)
    ends = [pair for k in range(groups) for pair in ((8 * k, 8 * k + 1), (8 * k + 7, 8 * k + 6))]
    shared = lax.ppermute(lax.dynamic_index_in_dim(blocks, 1 - core, 1, keepdims=False), "wide", ends)
    own = lax.dynamic_index_in_dim(blocks, core, 1, keepdims=False)
    first = chip == 0
    given = jnp.where(jnp.where(first, core == 0, core == 1), own, shared)
    before = after = jnp.zeros((COLS, ROWS), jnp.float32)
    for j in range(chips):
        back = chips - 1 - j
        pairs = []
        for k in range(groups - 1):
            for c in range(2):
                pairs.append((8 * k + 6 + c, 8 * (k + 1) + 2 * j + c))
                pairs.append((8 * (k + 1) + c, 8 * k + 2 * back + c))
        wanted = jnp.where(first, back, j)
        came = lax.ppermute(lax.dynamic_index_in_dim(given, wanted, 0, keepdims=False), "wide", pairs)
        before = jnp.where(chip == j, came, before)
        after = jnp.where(chip == back, came, after)
    return before, after


def local(distance, occupancy, material, colours, absorb, kernel_x, kernel_y):
    slices, col_count, row_count = distance.shape
    wide = lax.axis_size("wide")
    narrow = lax.axis_size("narrow")
    groups = wide // SLICES
    me = lax.axis_index("wide").astype(jnp.int32)
    core = (me & 1).reshape(1)
    members = [[SLICES * k + i for i in range(SLICES)] for k in range(groups)]

    def one(*shape):
        return jax.ShapeDtypeStruct(shape, jnp.float32)

    before, after = outer_blocks(distance, groups)
    message = pl.pallas_call(
        message_kernel,
        out_shape=one(BLOCKS, MESSAGE, ROWS),
        in_specs=[ANY] + [VMEM] * 2,
        out_specs=ANY,
        scratch_shapes=[
            pltpu.VMEM((col_count, ROWS), jnp.float32),
            pltpu.VMEM((BLOCKS, MESSAGE - COLS, ROWS), jnp.float32),
            pltpu.SemaphoreType.DMA((2, BLOCKS)),
        ],
        name="message",
    )(distance, jnp.swapaxes(material, 1, 2), jnp.swapaxes(occupancy, 1, 2))
    cells = lax.all_to_all(message, "wide", 0, 0, tiled=True, axis_index_groups=members)
    up = lax.ppermute(cells[:, COLS + 4 : COLS + 6], "narrow", [(i, i + 1) for i in range(narrow - 1)])
    down = lax.ppermute(cells[:, COLS + 2 : COLS + 4], "narrow", [(i + 1, i) for i in range(narrow - 1)])
    step = 4.0 / (slices * wide)
    fields = pl.pallas_call(
        functools.partial(fields_kernel, step),
        out_shape=[
            one(SLICES + 2, COLS, ROWS),
            one(SLICES, COLS, ROWS),
            one(SLICES, COLS, ROWS),
            one(FIELDS, SLICES, COLS // 8, ROWS),
        ],
        in_specs=[VMEM] * 3 + [SMEM] * 2 + [VMEM] * 2,
        out_specs=[VMEM] * 4,
        compiler_params=pltpu.CompilerParams(vmem_limit_bytes=24 * 1024 * 1024),
        cost_estimate=pl.CostEstimate(flops=4 * 10**9, bytes_accessed=6 * 1024 * 1024, transcendentals=0),
        name="fields",
    )(cells, before, after, colours, absorb, kernel_x, kernel_y)
    kept, given = pl.pallas_call(
        shade_kernel,
        out_shape=[one(CHIPS, FIELDS, PIECE, ROWS)] * 2,
        in_specs=[SMEM] + [VMEM] * 8,
        out_specs=[VMEM] * 2,
        scratch_shapes=[pltpu.VMEM((SLICES, COLS, ROWS), jnp.float32)],
        compiler_params=pltpu.CompilerParams(vmem_limit_bytes=24 * 1024 * 1024),
        name="shade",
    )(core, up, down, kernel_x, kernel_y, *fields)
    taken = lax.ppermute(given, "wide", [(i, i ^ 1) for i in range(wide)])
    along_z = [
        [32 * x + 2 * ((z + CHIPS * c) % 16) + c for z in range(16)] for x in range(wide // 32) for c in range(2)
    ]
    parts = lax.all_to_all(
        jnp.concatenate([kept, taken], axis=0), "wide", 0, 0, tiled=True, axis_index_groups=along_z
    )
    parts = parts.reshape(2, 2, 4, FIELDS, PIECE, ROWS)
    halves_z = [over(parts[h, 0], parts[h, 1]) for h in range(2)]
    front = core[0] == 0
    parts = over(jnp.where(front, halves_z[0], halves_z[1]), jnp.where(front, halves_z[1], halves_z[0]))
    along_x = [[32 * x + i for x in range(4)] for i in range(32)]
    parts = lax.all_to_all(parts, "wide", 0, 0, tiled=True, axis_index_groups=along_x)
    return over(over(parts[0], parts[1]), over(parts[2], parts[3]))


def solution(mesh):
    held = P("wide", None, "narrow")
    return jax.shard_map(
        local,
        mesh=mesh,
        in_specs=(held, held, held, P(), P(), P(), P()),
        out_specs=P(None, "wide", "narrow"),
        check_vma=False,
    )
```

```python
import functools

import jax
import jax.numpy as jnp
from jax import lax
from jax.experimental import pallas as pl
from jax.experimental.pallas import tpu as pltpu
from jax.sharding import PartitionSpec as P

BLOCKS = 8
SLICES = 8
COLS = 256
ROWS = 128
PIECE = 16
CHIPS = 8
MESSAGE = COLS + 16
FIELDS = 4
VMEM = pl.BlockSpec(memory_space=pltpu.VMEM)
SMEM = pl.BlockSpec(memory_space=pltpu.SMEM)
ANY = pl.BlockSpec(memory_space=pl.ANY)


def halves(value):
    high = value.astype(jnp.bfloat16)
    low = (value - high.astype(jnp.float32)).astype(jnp.bfloat16)
    return high, low


def product(a, b, dims=((1,), (0,))):
    a_high, a_low = a
    b_high, b_low = b

    def one(p, q):
        return lax.dot_general(p, q, (dims, ((), ())), preferred_element_type=jnp.float32)

    return one(a_high, b_high) + (one(a_low, b_high) + one(a_high, b_low))


def joined(a, b):
    a_high, a_low = a
    b_high, b_low = b
    return jnp.dot(
        jnp.concatenate([a_high, a_low, a_high], axis=1),
        jnp.concatenate([b_high, b_high, b_low], axis=0),
        preferred_element_type=jnp.float32,
    )


def ones_where(condition):
    return jnp.where(condition, 1.0, 0.0)


def iota(shape, dim):
    return lax.broadcasted_iota(jnp.int32, shape, dim)


def message_kernel(cells, material, occupancy, message, held, tail, sems):
    loads, stores = [], []
    for block in range(BLOCKS):
        part = held.at[block * COLS : (block + 1) * COLS]
        loads.append(pltpu.make_async_copy(cells.at[0, block * COLS : (block + 1) * COLS], part, sems.at[0, block]))
        stores.append(pltpu.make_async_copy(part, message.at[block, :COLS], sems.at[1, block]))
        loads[-1].start()
    brick_rows = material.shape[1]
    lane = iota((brick_rows, ROWS), 1)
    row = iota((brick_rows, ROWS), 0)
    kinds = material[0].astype(jnp.float32).T.reshape(BLOCKS, 4, 8, brick_rows)
    masks = occupancy[0].astype(jnp.float32).T.reshape(BLOCKS, 4, 8, brick_rows)
    packed = jnp.zeros((BLOCKS * 8, ROWS), jnp.float32)
    for part in range(4):
        at = 2 * brick_rows * part
        packed += jnp.dot(
            kinds[:, part].reshape(BLOCKS * 8, brick_rows),
            ones_where(lane == row + at),
            preferred_element_type=jnp.float32,
        )
        packed += jnp.dot(
            masks[:, part].reshape(BLOCKS * 8, brick_rows),
            ones_where(lane == row + (at + brick_rows)),
            preferred_element_type=jnp.float32,
        )
    ends = jnp.zeros((COLS, ROWS), jnp.float32)
    lane = iota((COLS, ROWS), 1)
    for block in range(BLOCKS):
        loads[block].wait()
        stores[block].start()
        turned = pltpu.roll(held[block * COLS : (block + 1) * COLS], 2 * block + 1, 1)
        ends = jnp.where(lane // 2 == block, turned, ends)
    ends = ends.T
    none = jnp.zeros((1, ROWS), jnp.float32)
    for block in range(BLOCKS):
        left, right = block * COLS, (block + 1) * COLS
        tail[block, 0:1] = held[left - 1 : left] if block else none
        tail[block, 1:2] = held[right : right + 1] if block < BLOCKS - 1 else none
        for end in range(2):
            row = 2 * block + 1 - end
            for part in range(2):
                at = 2 + 2 * end + part
                tail[block, at : at + 1] = ends[row : row + 1, part * ROWS : (part + 1) * ROWS]
        tail[block, 6:8] = jnp.zeros((2, ROWS), jnp.float32)
        tail[block, 8:16] = packed[block * 8 : block * 8 + 8]
    stores.append(pltpu.make_async_copy(tail, message.at[:, COLS:MESSAGE], sems.at[0, 0]))
    stores[-1].start()
    for store in stores:
        store.wait()


def weights(kernel):
    size = kernel.shape[0]
    return 0.5 * ones_where(iota((size, size), 0) == iota((size, size), 1)) + kernel[...]


def fields_kernel(
    step, cells, before, after, colours, absorb, kernel_x, kernel_y, distances, slopes_x, slopes_y, bricks
):
    along_x = halves(weights(kernel_x).T)
    along_y = weights(kernel_y)
    none = jnp.zeros((1, ROWS), jnp.float32)
    slope_y = 0.5 * (
        jnp.concatenate([none, along_y[:-1]], axis=0) - jnp.concatenate([along_y[1:], none], axis=0)
    )
    only_y = halves(along_y)
    both_y = halves(jnp.concatenate([along_y, slope_y], axis=1))
    column_ends = jnp.concatenate([cells[s, COLS : COLS + 2] for s in range(SLICES)], axis=0)
    column_ends = product(halves(column_ends), only_y)
    outer = joined(halves(jnp.concatenate([before[...], after[...]], axis=0)), only_y)
    outer = jnp.concatenate([outer[:COLS], outer[COLS:]], axis=1)
    outer = joined(along_x, halves(outer))
    distances[0] = outer[:, :ROWS]
    distances[SLICES + 1] = outer[:, ROWS:]
    for pair in range(SLICES // 2):
        parts = []
        for s in (2 * pair, 2 * pair + 1):
            rows = joined(halves(cells[s, :COLS]), both_y)
            value = rows[:, :ROWS]
            ahead = jnp.concatenate([value[1:], column_ends[2 * s + 1 : 2 * s + 2]], axis=0)
            behind = jnp.concatenate([column_ends[2 * s : 2 * s + 1], value[:-1]], axis=0)
            parts += [value, 0.5 * (ahead - behind), rows[:, ROWS:]]
        mixed = joined(along_x, halves(jnp.concatenate(parts, axis=1)))
        for i, s in enumerate((2 * pair, 2 * pair + 1)):
            at = 3 * i * ROWS
            distances[1 + s] = mixed[:, at : at + ROWS]
            slopes_x[s] = mixed[:, at + ROWS : at + 2 * ROWS]
            slopes_y[s] = mixed[:, at + 2 * ROWS : at + 3 * ROWS]
    codes = cells[:, COLS + 8 : MESSAGE, :].reshape(SLICES * 8, ROWS)
    brick_rows = ROWS // 8
    masks = pltpu.roll(codes, ROWS - brick_rows, 1)
    values = [jnp.zeros_like(codes)] * FIELDS
    for label in range(colours.shape[1]):
        found = codes == float(label)
        for f in range(FIELDS):
            entry = colours[f, label] if f < 3 else absorb[label]
            values[f] = jnp.where(found, entry, values[f])
    values[3] = values[3] * masks * step
    values = jnp.concatenate(values, axis=0)
    source = iota((ROWS, 4 * ROWS), 0)
    target = iota((ROWS, 4 * ROWS), 1)
    spread = ones_where(source == (target // ROWS) * (2 * brick_rows) + (target % ROWS) // 8)
    spread = spread.astype(jnp.bfloat16)
    high, low = halves(values)
    least = (values - high.astype(jnp.float32) - low.astype(jnp.float32)).astype(jnp.bfloat16)
    grown = (
        jnp.dot(least, spread, preferred_element_type=jnp.float32)
        + jnp.dot(low, spread, preferred_element_type=jnp.float32)
        + jnp.dot(high, spread, preferred_element_type=jnp.float32)
    )
    for f in range(FIELDS):
        for s in range(SLICES):
            for part in range(4):
                bricks[f, s, 8 * part : 8 * part + 8] = grown[
                    (f * SLICES + s) * 8 : (f * SLICES + s) * 8 + 8, part * ROWS : (part + 1) * ROWS
                ]


def shade(core, distances, slopes_x, slopes_y, edges, bricks, image):
    def tile(chip, part):
        row = (2 * chip + core) * (PIECE // 8) + part
        at = pl.ds(pl.multiple_of(row * 8, 8), 8)
        brick = pl.ds(row, 1)
        transmit = jnp.ones((8, ROWS), jnp.float32)
        total = [jnp.zeros((8, ROWS), jnp.float32)] * FIELDS
        d_of = [distances[s, at] for s in range(SLICES + 2)]
        for s in range(SLICES):
            d = d_of[1 + s]
            u = slopes_x[s, at]
            v = slopes_y[s, at] + edges[s, at]
            w = 0.5 * (d_of[2 + s] - d_of[s])
            norm = jnp.maximum(u * u + v * v + w * w, 0.1)
            facing = 0.25 + 0.75 * jnp.abs(w) * lax.rsqrt(norm)
            density = jnp.exp(-2.0 * d * d)
            opacity = 1.0 - jnp.exp(-bricks[3, s, brick] * density)
            weight = transmit * opacity
            shaded = weight * facing
            for f in range(3):
                total[f] = total[f] + shaded * bricks[f, s, brick]
            total[3] = total[3] + weight
            transmit = transmit * (1.0 - opacity)
        for f in range(FIELDS):
            image[chip, f, 8 * part : 8 * part + 8] = total[f]

    def two(i, _):
        for chip in (2 * i, 2 * i + 1):
            for part in range(PIECE // 8):
                tile(chip, part)
        return 0

    lax.fori_loop(0, CHIPS // 2, two, 0)


def given_kernel(core, up, down, kernel_x, kernel_y, distances, slopes_x, slopes_y, bricks, given, edges):
    beside = jnp.concatenate(
        [
            jnp.concatenate([rows[s, 0:1], rows[s, 1:2]], axis=1)
            for s in range(SLICES)
            for rows in (up, down)
        ],
        axis=0,
    )
    beside = halves(product(halves(beside), halves(weights(kernel_x))).T)
    along_y = weights(kernel_y)
    row = iota((2 * SLICES, ROWS), 0)
    for s in range(SLICES):
        wanted = jnp.where(row == 2 * s, -0.5 * along_y[0:1], 0.0) + jnp.where(
            row == 2 * s + 1, 0.5 * along_y[ROWS - 1 : ROWS], 0.0
        )
        edges[s] = product(beside, halves(wanted))
    shade(1 - core[0], distances, slopes_x, slopes_y, edges, bricks, given)


def kept_kernel(core, distances, slopes_x, slopes_y, bricks, edges, kept):
    shade(core[0], distances, slopes_x, slopes_y, edges, bricks, kept)


def over(nearer, farther):
    return nearer + (1.0 - nearer[..., 3:4, :, :]) * farther


def outer_blocks(distance, groups):
    chips = SLICES // 2
    me = lax.axis_index("wide")
    chip, core = me % SLICES // 2, me % 2
    blocks = distance.reshape(chips, 2, COLS, ROWS)
    ends = [pair for k in range(groups) for pair in ((8 * k, 8 * k + 1), (8 * k + 7, 8 * k + 6))]
    shared = lax.ppermute(lax.dynamic_index_in_dim(blocks, 1 - core, 1, keepdims=False), "wide", ends)
    own = lax.dynamic_index_in_dim(blocks, core, 1, keepdims=False)
    first = chip == 0
    given = jnp.where(jnp.where(first, core == 0, core == 1), own, shared)
    before = after = jnp.zeros((COLS, ROWS), jnp.float32)
    for j in range(chips):
        back = chips - 1 - j
        pairs = []
        for k in range(groups - 1):
            for c in range(2):
                pairs.append((8 * k + 6 + c, 8 * (k + 1) + 2 * j + c))
                pairs.append((8 * (k + 1) + c, 8 * k + 2 * back + c))
        wanted = jnp.where(first, back, j)
        came = lax.ppermute(lax.dynamic_index_in_dim(given, wanted, 0, keepdims=False), "wide", pairs)
        before = jnp.where(chip == j, came, before)
        after = jnp.where(chip == back, came, after)
    return before, after


def local(distance, occupancy, material, colours, absorb, kernel_x, kernel_y):
    slices, col_count, row_count = distance.shape
    wide = lax.axis_size("wide")
    narrow = lax.axis_size("narrow")
    groups = wide // SLICES
    me = lax.axis_index("wide").astype(jnp.int32)
    core = (me & 1).reshape(1)
    members = [[SLICES * k + i for i in range(SLICES)] for k in range(groups)]

    def one(*shape):
        return jax.ShapeDtypeStruct(shape, jnp.float32)

    before, after = outer_blocks(distance, groups)
    message = pl.pallas_call(
        message_kernel,
        out_shape=one(BLOCKS, MESSAGE, ROWS),
        in_specs=[ANY] + [VMEM] * 2,
        out_specs=ANY,
        scratch_shapes=[
            pltpu.VMEM((col_count, ROWS), jnp.float32),
            pltpu.VMEM((BLOCKS, MESSAGE - COLS, ROWS), jnp.float32),
            pltpu.SemaphoreType.DMA((2, BLOCKS)),
        ],
        name="message",
    )(distance, jnp.swapaxes(material, 1, 2), jnp.swapaxes(occupancy, 1, 2))
    cells = lax.all_to_all(message, "wide", 0, 0, tiled=True, axis_index_groups=members)
    up = lax.ppermute(cells[:, COLS + 4 : COLS + 6], "narrow", [(i, i + 1) for i in range(narrow - 1)])
    down = lax.ppermute(cells[:, COLS + 2 : COLS + 4], "narrow", [(i + 1, i) for i in range(narrow - 1)])
    step = 4.0 / (slices * wide)
    fields = pl.pallas_call(
        functools.partial(fields_kernel, step),
        out_shape=[
            one(SLICES + 2, COLS, ROWS),
            one(SLICES, COLS, ROWS),
            one(SLICES, COLS, ROWS),
            one(FIELDS, SLICES, COLS // 8, ROWS),
        ],
        in_specs=[VMEM] * 3 + [SMEM] * 2 + [VMEM] * 2,
        out_specs=[VMEM] * 4,
        compiler_params=pltpu.CompilerParams(vmem_limit_bytes=24 * 1024 * 1024),
        cost_estimate=pl.CostEstimate(flops=4 * 10**9, bytes_accessed=6 * 1024 * 1024, transcendentals=0),
        name="fields",
    )(cells, before, after, colours, absorb, kernel_x, kernel_y)
    params = pltpu.CompilerParams(vmem_limit_bytes=24 * 1024 * 1024)
    half = one(CHIPS, FIELDS, PIECE, ROWS)
    given, edges = pl.pallas_call(
        given_kernel,
        out_shape=[half, one(SLICES, COLS, ROWS)],
        in_specs=[SMEM] + [VMEM] * 8,
        out_specs=[VMEM] * 2,
        compiler_params=params,
        name="given",
    )(core, up, down, kernel_x, kernel_y, *fields)
    taken = lax.ppermute(given, "wide", [(i, i ^ 1) for i in range(wide)])
    taken, front = lax.optimization_barrier((taken, jnp.broadcast_to(core == 0, (PIECE, ROWS))))
    kept = pl.pallas_call(
        kept_kernel,
        out_shape=half,
        in_specs=[SMEM] + [VMEM] * 5,
        out_specs=VMEM,
        compiler_params=params,
        cost_estimate=pl.CostEstimate(flops=10**8, bytes_accessed=6 * 1024 * 1024, transcendentals=0),
        name="kept",
    )(core, *fields, edges)
    along_z = [
        [32 * x + 2 * ((z + CHIPS * c) % 16) + c for z in range(16)] for x in range(wide // 32) for c in range(2)
    ]
    parts = lax.all_to_all(
        jnp.concatenate([kept, taken], axis=0), "wide", 0, 0, tiled=True, axis_index_groups=along_z
    )
    parts = parts.reshape(2, 2, 4, FIELDS, PIECE, ROWS)
    halves_z = [over(parts[h, 0], parts[h, 1]) for h in range(2)]
    parts = over(jnp.where(front, halves_z[0], halves_z[1]), jnp.where(front, halves_z[1], halves_z[0]))
    along_x = [[32 * x + i for x in range(4)] for i in range(32)]
    parts = lax.all_to_all(parts, "wide", 0, 0, tiled=True, axis_index_groups=along_x)
    return over(over(parts[0], parts[1]), over(parts[2], parts[3]))


def solution(mesh):
    held = P("wide", None, "narrow")
    return jax.shard_map(
        local,
        mesh=mesh,
        in_specs=(held, held, held, P(), P(), P(), P()),
        out_specs=P(None, "wide", "narrow"),
        check_vma=False,
    )
```

```python
import functools

import jax
import jax.numpy as jnp
from jax import lax
from jax.experimental import pallas as pl
from jax.experimental.pallas import tpu as pltpu
from jax.sharding import PartitionSpec as P

BLOCKS = 8
SLICES = 8
COLS = 256
ROWS = 128
PIECE = 16
CHIPS = 8
MESSAGE = COLS + 16
FIELDS = 4
VMEM = pl.BlockSpec(memory_space=pltpu.VMEM)
SMEM = pl.BlockSpec(memory_space=pltpu.SMEM)
ANY = pl.BlockSpec(memory_space=pl.ANY)


def halves(value):
    high = value.astype(jnp.bfloat16)
    low = (value - high.astype(jnp.float32)).astype(jnp.bfloat16)
    return high, low


def product(a, b, dims=((1,), (0,))):
    a_high, a_low = a
    b_high, b_low = b

    def one(p, q):
        return lax.dot_general(p, q, (dims, ((), ())), preferred_element_type=jnp.float32)

    return one(a_high, b_high) + (one(a_low, b_high) + one(a_high, b_low))


def joined(a, b):
    a_high, a_low = a
    b_high, b_low = b
    return jnp.dot(
        jnp.concatenate([a_high, a_low, a_high], axis=1),
        jnp.concatenate([b_high, b_high, b_low], axis=0),
        preferred_element_type=jnp.float32,
    )


def ones_where(condition):
    return jnp.where(condition, 1.0, 0.0)


def iota(shape, dim):
    return lax.broadcasted_iota(jnp.int32, shape, dim)


def message_kernel(cells, material_in, occupancy_in, message, held, tail, material, occupancy, sems):
    loads, stores = [], []
    brick_loads = [
        pltpu.make_async_copy(material_in, material, sems.at[0, BLOCKS]),
        pltpu.make_async_copy(occupancy_in, occupancy, sems.at[1, BLOCKS]),
    ]
    for load in brick_loads:
        load.start()
    for block in range(BLOCKS):
        part = held.at[block * COLS : (block + 1) * COLS]
        loads.append(pltpu.make_async_copy(cells.at[0, block * COLS : (block + 1) * COLS], part, sems.at[0, block]))
        stores.append(pltpu.make_async_copy(part, message.at[block, :COLS], sems.at[1, block]))
        loads[-1].start()
    for load in brick_loads:
        load.wait()
    brick_rows = material.shape[1]
    lane = iota((brick_rows, ROWS), 1)
    row = iota((brick_rows, ROWS), 0)
    kinds = material[0].astype(jnp.float32).T.reshape(BLOCKS, 4, 8, brick_rows)
    masks = occupancy[0].astype(jnp.float32).T.reshape(BLOCKS, 4, 8, brick_rows)
    packed = jnp.zeros((BLOCKS * 8, ROWS), jnp.float32)
    for part in range(4):
        at = 2 * brick_rows * part
        packed += jnp.dot(
            kinds[:, part].reshape(BLOCKS * 8, brick_rows),
            ones_where(lane == row + at),
            preferred_element_type=jnp.float32,
        )
        packed += jnp.dot(
            masks[:, part].reshape(BLOCKS * 8, brick_rows),
            ones_where(lane == row + (at + brick_rows)),
            preferred_element_type=jnp.float32,
        )
    ends = jnp.zeros((COLS, ROWS), jnp.float32)
    lane = iota((COLS, ROWS), 1)
    for block in range(BLOCKS):
        loads[block].wait()
        stores[block].start()
        turned = pltpu.roll(held[block * COLS : (block + 1) * COLS], 2 * block + 1, 1)
        ends = jnp.where(lane // 2 == block, turned, ends)
    ends = ends.T
    none = jnp.zeros((1, ROWS), jnp.float32)
    for block in range(BLOCKS):
        left, right = block * COLS, (block + 1) * COLS
        tail[block, 0:1] = held[left - 1 : left] if block else none
        tail[block, 1:2] = held[right : right + 1] if block < BLOCKS - 1 else none
        for end in range(2):
            row = 2 * block + 1 - end
            for part in range(2):
                at = 2 + 2 * end + part
                tail[block, at : at + 1] = ends[row : row + 1, part * ROWS : (part + 1) * ROWS]
        tail[block, 6:8] = jnp.zeros((2, ROWS), jnp.float32)
        tail[block, 8:16] = packed[block * 8 : block * 8 + 8]
    stores.append(pltpu.make_async_copy(tail, message.at[:, COLS:MESSAGE], sems.at[0, 0]))
    stores[-1].start()
    for store in stores:
        store.wait()


def weights(kernel):
    size = kernel.shape[0]
    return 0.5 * ones_where(iota((size, size), 0) == iota((size, size), 1)) + kernel[...]


def fields_kernel(
    step, cells, before, after, colours, absorb, kernel_x, kernel_y, distances, slopes_x, slopes_y, bricks
):
    along_x = halves(weights(kernel_x).T)
    along_y = weights(kernel_y)
    none = jnp.zeros((1, ROWS), jnp.float32)
    slope_y = 0.5 * (
        jnp.concatenate([none, along_y[:-1]], axis=0) - jnp.concatenate([along_y[1:], none], axis=0)
    )
    only_y = halves(along_y)
    both_y = halves(jnp.concatenate([along_y, slope_y], axis=1))
    column_ends = jnp.concatenate([cells[s, COLS : COLS + 2] for s in range(SLICES)], axis=0)
    column_ends = product(halves(column_ends), only_y)
    outer = joined(halves(jnp.concatenate([before[...], after[...]], axis=0)), only_y)
    outer = jnp.concatenate([outer[:COLS], outer[COLS:]], axis=1)
    outer = joined(along_x, halves(outer))
    distances[0] = outer[:, :ROWS]
    distances[SLICES + 1] = outer[:, ROWS:]
    for pair in range(SLICES // 2):
        parts = []
        for s in (2 * pair, 2 * pair + 1):
            rows = joined(halves(cells[s, :COLS]), both_y)
            value = rows[:, :ROWS]
            ahead = jnp.concatenate([value[1:], column_ends[2 * s + 1 : 2 * s + 2]], axis=0)
            behind = jnp.concatenate([column_ends[2 * s : 2 * s + 1], value[:-1]], axis=0)
            parts += [value, 0.5 * (ahead - behind), rows[:, ROWS:]]
        mixed = joined(along_x, halves(jnp.concatenate(parts, axis=1)))
        for i, s in enumerate((2 * pair, 2 * pair + 1)):
            at = 3 * i * ROWS
            distances[1 + s] = mixed[:, at : at + ROWS]
            slopes_x[s] = mixed[:, at + ROWS : at + 2 * ROWS]
            slopes_y[s] = mixed[:, at + 2 * ROWS : at + 3 * ROWS]
    codes = cells[:, COLS + 8 : MESSAGE, :].reshape(SLICES * 8, ROWS)
    brick_rows = ROWS // 8
    masks = pltpu.roll(codes, ROWS - brick_rows, 1)
    values = [jnp.zeros_like(codes)] * FIELDS
    for label in range(colours.shape[1]):
        found = codes == float(label)
        for f in range(FIELDS):
            entry = colours[f, label] if f < 3 else absorb[label]
            values[f] = jnp.where(found, entry, values[f])
    values[3] = values[3] * masks * step
    values = jnp.concatenate(values, axis=0)
    source = iota((ROWS, 4 * ROWS), 0)
    target = iota((ROWS, 4 * ROWS), 1)
    spread = ones_where(source == (target // ROWS) * (2 * brick_rows) + (target % ROWS) // 8)
    spread = spread.astype(jnp.bfloat16)
    high, low = halves(values)
    least = (values - high.astype(jnp.float32) - low.astype(jnp.float32)).astype(jnp.bfloat16)
    grown = (
        jnp.dot(least, spread, preferred_element_type=jnp.float32)
        + jnp.dot(low, spread, preferred_element_type=jnp.float32)
        + jnp.dot(high, spread, preferred_element_type=jnp.float32)
    )
    for f in range(FIELDS):
        for s in range(SLICES):
            for part in range(4):
                bricks[f, s, 8 * part : 8 * part + 8] = grown[
                    (f * SLICES + s) * 8 : (f * SLICES + s) * 8 + 8, part * ROWS : (part + 1) * ROWS
                ]


def shade(core, distances, slopes_x, slopes_y, edges, bricks, image):
    def tile(chip, part):
        row = (2 * chip + core) * (PIECE // 8) + part
        at = pl.ds(pl.multiple_of(row * 8, 8), 8)
        brick = pl.ds(row, 1)
        transmit = jnp.ones((8, ROWS), jnp.float32)
        total = [jnp.zeros((8, ROWS), jnp.float32)] * FIELDS
        d_of = [distances[s, at] for s in range(SLICES + 2)]
        for s in range(SLICES):
            d = d_of[1 + s]
            u = slopes_x[s, at]
            v = slopes_y[s, at] + edges[s, at]
            w = 0.5 * (d_of[2 + s] - d_of[s])
            norm = jnp.maximum(u * u + v * v + w * w, 0.1)
            facing = 0.25 + 0.75 * jnp.abs(w) * lax.rsqrt(norm)
            density = jnp.exp(-2.0 * d * d)
            opacity = 1.0 - jnp.exp(-bricks[3, s, brick] * density)
            weight = transmit * opacity
            shaded = weight * facing
            for f in range(3):
                total[f] = total[f] + shaded * bricks[f, s, brick]
            total[3] = total[3] + weight
            transmit = transmit * (1.0 - opacity)
        for f in range(FIELDS):
            image[chip, f, 8 * part : 8 * part + 8] = total[f]

    def two(i, _):
        for chip in (2 * i, 2 * i + 1):
            for part in range(PIECE // 8):
                tile(chip, part)
        return 0

    lax.fori_loop(0, CHIPS // 2, two, 0)


def given_kernel(core, up, down, kernel_x, kernel_y, distances, slopes_x, slopes_y, bricks, given, edges):
    beside = jnp.concatenate(
        [
            jnp.concatenate([rows[s, 0:1], rows[s, 1:2]], axis=1)
            for s in range(SLICES)
            for rows in (up, down)
        ],
        axis=0,
    )
    beside = halves(product(halves(beside), halves(weights(kernel_x))).T)
    along_y = weights(kernel_y)
    row = iota((2 * SLICES, ROWS), 0)
    for s in range(SLICES):
        wanted = jnp.where(row == 2 * s, -0.5 * along_y[0:1], 0.0) + jnp.where(
            row == 2 * s + 1, 0.5 * along_y[ROWS - 1 : ROWS], 0.0
        )
        edges[s] = product(beside, halves(wanted))
    shade(1 - core[0], distances, slopes_x, slopes_y, edges, bricks, given)


def kept_kernel(core, distances, slopes_x, slopes_y, bricks, edges, kept):
    shade(core[0], distances, slopes_x, slopes_y, edges, bricks, kept)


def over(nearer, farther):
    return nearer + (1.0 - nearer[..., 3:4, :, :]) * farther


def outer_blocks(distance, groups):
    chips = SLICES // 2
    me = lax.axis_index("wide")
    chip, core = me % SLICES // 2, me % 2
    blocks = distance.reshape(chips, 2, COLS, ROWS)
    ends = [pair for k in range(groups) for pair in ((8 * k, 8 * k + 1), (8 * k + 7, 8 * k + 6))]
    shared = lax.ppermute(lax.dynamic_index_in_dim(blocks, 1 - core, 1, keepdims=False), "wide", ends)
    own = lax.dynamic_index_in_dim(blocks, core, 1, keepdims=False)
    first = chip == 0
    given = jnp.where(jnp.where(first, core == 0, core == 1), own, shared)
    before = after = jnp.zeros((COLS, ROWS), jnp.float32)
    for j in range(chips):
        back = chips - 1 - j
        pairs = []
        for k in range(groups - 1):
            for c in range(2):
                pairs.append((8 * k + 6 + c, 8 * (k + 1) + 2 * j + c))
                pairs.append((8 * (k + 1) + c, 8 * k + 2 * back + c))
        wanted = jnp.where(first, back, j)
        came = lax.ppermute(lax.dynamic_index_in_dim(given, wanted, 0, keepdims=False), "wide", pairs)
        before = jnp.where(chip == j, came, before)
        after = jnp.where(chip == back, came, after)
    return before, after


def local(distance, occupancy, material, colours, absorb, kernel_x, kernel_y):
    slices, col_count, row_count = distance.shape
    wide = lax.axis_size("wide")
    narrow = lax.axis_size("narrow")
    groups = wide // SLICES
    me = lax.axis_index("wide").astype(jnp.int32)
    core = (me & 1).reshape(1)
    members = [[SLICES * k + i for i in range(SLICES)] for k in range(groups)]

    def one(*shape):
        return jax.ShapeDtypeStruct(shape, jnp.float32)

    before, after = outer_blocks(distance, groups)
    message = pl.pallas_call(
        message_kernel,
        out_shape=one(BLOCKS, MESSAGE, ROWS),
        in_specs=[ANY] * 3,
        out_specs=ANY,
        scratch_shapes=[
            pltpu.VMEM((col_count, ROWS), jnp.float32),
            pltpu.VMEM((BLOCKS, MESSAGE - COLS, ROWS), jnp.float32),
            pltpu.VMEM((1, material.shape[2], material.shape[1]), jnp.int32),
            pltpu.VMEM((1, material.shape[2], material.shape[1]), jnp.int32),
            pltpu.SemaphoreType.DMA((2, BLOCKS + 1)),
        ],
        name="message",
    )(distance, jnp.swapaxes(material, 1, 2), jnp.swapaxes(occupancy, 1, 2))
    cells = lax.all_to_all(message, "wide", 0, 0, tiled=True, axis_index_groups=members)
    up = lax.ppermute(cells[:, COLS + 4 : COLS + 6], "narrow", [(i, i + 1) for i in range(narrow - 1)])
    down = lax.ppermute(cells[:, COLS + 2 : COLS + 4], "narrow", [(i + 1, i) for i in range(narrow - 1)])
    step = 4.0 / (slices * wide)
    fields = pl.pallas_call(
        functools.partial(fields_kernel, step),
        out_shape=[
            one(SLICES + 2, COLS, ROWS),
            one(SLICES, COLS, ROWS),
            one(SLICES, COLS, ROWS),
            one(FIELDS, SLICES, COLS // 8, ROWS),
        ],
        in_specs=[VMEM] * 3 + [SMEM] * 2 + [VMEM] * 2,
        out_specs=[VMEM] * 4,
        compiler_params=pltpu.CompilerParams(vmem_limit_bytes=24 * 1024 * 1024),
        cost_estimate=pl.CostEstimate(flops=4 * 10**9, bytes_accessed=6 * 1024 * 1024, transcendentals=0),
        name="fields",
    )(cells, before, after, colours, absorb, kernel_x, kernel_y)
    params = pltpu.CompilerParams(vmem_limit_bytes=24 * 1024 * 1024)
    half = one(CHIPS, FIELDS, PIECE, ROWS)
    given, edges = pl.pallas_call(
        given_kernel,
        out_shape=[half, one(SLICES, COLS, ROWS)],
        in_specs=[SMEM] + [VMEM] * 8,
        out_specs=[VMEM] * 2,
        compiler_params=params,
        name="given",
    )(core, up, down, kernel_x, kernel_y, *fields)
    taken = lax.ppermute(given, "wide", [(i, i ^ 1) for i in range(wide)])
    taken, front = lax.optimization_barrier((taken, jnp.broadcast_to(core == 0, (PIECE, ROWS))))
    kept = pl.pallas_call(
        kept_kernel,
        out_shape=half,
        in_specs=[SMEM] + [VMEM] * 5,
        out_specs=VMEM,
        compiler_params=params,
        cost_estimate=pl.CostEstimate(flops=10**8, bytes_accessed=6 * 1024 * 1024, transcendentals=0),
        name="kept",
    )(core, *fields, edges)
    along_z = [
        [32 * x + 2 * ((z + CHIPS * c) % 16) + c for z in range(16)] for x in range(wide // 32) for c in range(2)
    ]
    parts = lax.all_to_all(
        jnp.concatenate([kept, taken], axis=0), "wide", 0, 0, tiled=True, axis_index_groups=along_z
    )
    parts = parts.reshape(2, 2, 4, FIELDS, PIECE, ROWS)
    halves_z = [over(parts[h, 0], parts[h, 1]) for h in range(2)]
    parts = over(jnp.where(front, halves_z[0], halves_z[1]), jnp.where(front, halves_z[1], halves_z[0]))
    along_x = [[32 * x + i for x in range(4)] for i in range(32)]
    parts = lax.all_to_all(parts, "wide", 0, 0, tiled=True, axis_index_groups=along_x)
    return over(over(parts[0], parts[1]), over(parts[2], parts[3]))


def solution(mesh):
    held = P("wide", None, "narrow")
    return jax.shard_map(
        local,
        mesh=mesh,
        in_specs=(held, held, held, P(), P(), P(), P()),
        out_specs=P(None, "wide", "narrow"),
        check_vma=False,
    )
```

```python
import functools

import jax
import jax.numpy as jnp
from jax import lax
from jax.experimental import pallas as pl
from jax.experimental.pallas import tpu as pltpu
from jax.sharding import PartitionSpec as P

BLOCKS = 8
SLICES = 8
COLS = 256
ROWS = 128
PIECE = 16
CHIPS = 8
MESSAGE = COLS + 16
FIELDS = 4
VMEM = pl.BlockSpec(memory_space=pltpu.VMEM)
SMEM = pl.BlockSpec(memory_space=pltpu.SMEM)
ANY = pl.BlockSpec(memory_space=pl.ANY)


def halves(value):
    high = value.astype(jnp.bfloat16)
    low = (value - high.astype(jnp.float32)).astype(jnp.bfloat16)
    return high, low


def product(a, b, dims=((1,), (0,))):
    a_high, a_low = a
    b_high, b_low = b

    def one(p, q):
        return lax.dot_general(p, q, (dims, ((), ())), preferred_element_type=jnp.float32)

    return one(a_high, b_high) + (one(a_low, b_high) + one(a_high, b_low))


def joined(a, b):
    a_high, a_low = a
    b_high, b_low = b
    return jnp.dot(
        jnp.concatenate([a_high, a_low, a_high], axis=1),
        jnp.concatenate([b_high, b_high, b_low], axis=0),
        preferred_element_type=jnp.float32,
    )


def ones_where(condition):
    return jnp.where(condition, 1.0, 0.0)


def iota(shape, dim):
    return lax.broadcasted_iota(jnp.int32, shape, dim)


def message_kernel(cells, material_in, occupancy_in, message, held, tail, material, occupancy, sems):
    loads, stores = [], []
    brick_loads = [
        pltpu.make_async_copy(material_in, material, sems.at[0, BLOCKS]),
        pltpu.make_async_copy(occupancy_in, occupancy, sems.at[1, BLOCKS]),
    ]
    for load in brick_loads:
        load.start()
    for block in range(BLOCKS):
        part = held.at[block * COLS : (block + 1) * COLS]
        loads.append(pltpu.make_async_copy(cells.at[0, block * COLS : (block + 1) * COLS], part, sems.at[0, block]))
        stores.append(pltpu.make_async_copy(part, message.at[block, :COLS], sems.at[1, block]))
        loads[-1].start()
    for load in brick_loads:
        load.wait()
    brick_rows = material.shape[1]
    lane = iota((brick_rows, ROWS), 1)
    row = iota((brick_rows, ROWS), 0)
    kinds = material[0].astype(jnp.float32).T.reshape(BLOCKS, 4, 8, brick_rows)
    masks = occupancy[0].astype(jnp.float32).T.reshape(BLOCKS, 4, 8, brick_rows)
    packed = jnp.zeros((BLOCKS * 8, ROWS), jnp.float32)
    for part in range(4):
        at = 2 * brick_rows * part
        packed += jnp.dot(
            kinds[:, part].reshape(BLOCKS * 8, brick_rows),
            ones_where(lane == row + at),
            preferred_element_type=jnp.float32,
        )
        packed += jnp.dot(
            masks[:, part].reshape(BLOCKS * 8, brick_rows),
            ones_where(lane == row + (at + brick_rows)),
            preferred_element_type=jnp.float32,
        )
    ends = jnp.zeros((COLS, ROWS), jnp.float32)
    lane = iota((COLS, ROWS), 1)
    for block in range(BLOCKS):
        loads[block].wait()
        stores[block].start()
        turned = pltpu.roll(held[block * COLS : (block + 1) * COLS], 2 * block + 1, 1)
        ends = jnp.where(lane // 2 == block, turned, ends)
    ends = ends.T
    none = jnp.zeros((1, ROWS), jnp.float32)
    for block in range(BLOCKS):
        left, right = block * COLS, (block + 1) * COLS
        tail[block, 0:1] = held[left - 1 : left] if block else none
        tail[block, 1:2] = held[right : right + 1] if block < BLOCKS - 1 else none
        for end in range(2):
            row = 2 * block + 1 - end
            for part in range(2):
                at = 2 + 2 * end + part
                tail[block, at : at + 1] = ends[row : row + 1, part * ROWS : (part + 1) * ROWS]
        tail[block, 6:8] = jnp.zeros((2, ROWS), jnp.float32)
        tail[block, 8:16] = packed[block * 8 : block * 8 + 8]
    stores.append(pltpu.make_async_copy(tail, message.at[:, COLS:MESSAGE], sems.at[0, 0]))
    stores[-1].start()
    for store in stores:
        store.wait()


def weights(kernel):
    size = kernel.shape[0]
    return 0.5 * ones_where(iota((size, size), 0) == iota((size, size), 1)) + kernel[...]


def fields_kernel(
    step, cells, before, after, colours, absorb, kernel_x, kernel_y, distances, slopes_x, slopes_y, bricks
):
    along_x = halves(weights(kernel_x).T)
    along_y = weights(kernel_y)
    none = jnp.zeros((1, ROWS), jnp.float32)
    slope_y = 0.5 * (
        jnp.concatenate([none, along_y[:-1]], axis=0) - jnp.concatenate([along_y[1:], none], axis=0)
    )
    only_y = halves(along_y)
    both_y = halves(jnp.concatenate([along_y, slope_y], axis=1))
    column_ends = jnp.concatenate([cells[s, COLS : COLS + 2] for s in range(SLICES)], axis=0)
    column_ends = product(halves(column_ends), only_y)
    outer = joined(halves(jnp.concatenate([before[...], after[...]], axis=0)), only_y)
    outer = jnp.concatenate([outer[:COLS], outer[COLS:]], axis=1)
    outer = joined(along_x, halves(outer))
    distances[0] = outer[:, :ROWS]
    distances[SLICES + 1] = outer[:, ROWS:]
    for pair in range(SLICES // 2):
        parts = []
        for s in (2 * pair, 2 * pair + 1):
            rows = joined(halves(cells[s, :COLS]), both_y)
            value = rows[:, :ROWS]
            ahead = jnp.concatenate([value[1:], column_ends[2 * s + 1 : 2 * s + 2]], axis=0)
            behind = jnp.concatenate([column_ends[2 * s : 2 * s + 1], value[:-1]], axis=0)
            parts += [value, 0.5 * (ahead - behind), rows[:, ROWS:]]
        mixed = joined(along_x, halves(jnp.concatenate(parts, axis=1)))
        for i, s in enumerate((2 * pair, 2 * pair + 1)):
            at = 3 * i * ROWS
            distances[1 + s] = mixed[:, at : at + ROWS]
            slopes_x[s] = mixed[:, at + ROWS : at + 2 * ROWS]
            slopes_y[s] = mixed[:, at + 2 * ROWS : at + 3 * ROWS]
    codes = cells[:, COLS + 8 : MESSAGE, :].reshape(SLICES * 8, ROWS)
    brick_rows = ROWS // 8
    masks = pltpu.roll(codes, ROWS - brick_rows, 1)
    values = [jnp.zeros_like(codes)] * FIELDS
    for label in range(colours.shape[1]):
        found = codes == float(label)
        for f in range(FIELDS):
            entry = colours[f, label] if f < 3 else absorb[label]
            values[f] = jnp.where(found, entry, values[f])
    values[3] = values[3] * masks * step
    values = jnp.concatenate(values, axis=0)
    source = iota((ROWS, 4 * ROWS), 0)
    target = iota((ROWS, 4 * ROWS), 1)
    spread = ones_where(source == (target // ROWS) * (2 * brick_rows) + (target % ROWS) // 8)
    spread = spread.astype(jnp.bfloat16)
    high, low = halves(values)
    least = (values - high.astype(jnp.float32) - low.astype(jnp.float32)).astype(jnp.bfloat16)
    grown = (
        jnp.dot(least, spread, preferred_element_type=jnp.float32)
        + jnp.dot(low, spread, preferred_element_type=jnp.float32)
        + jnp.dot(high, spread, preferred_element_type=jnp.float32)
    )
    for f in range(FIELDS):
        for s in range(SLICES):
            for part in range(4):
                bricks[f, s, 8 * part : 8 * part + 8] = grown[
                    (f * SLICES + s) * 8 : (f * SLICES + s) * 8 + 8, part * ROWS : (part + 1) * ROWS
                ]


def shade(core, distances, slopes_x, slopes_y, edges, bricks, image):
    def tile(chip, part):
        row = (2 * chip + core) * (PIECE // 8) + part
        at = pl.ds(pl.multiple_of(row * 8, 8), 8)
        brick = pl.ds(row, 1)
        transmit = jnp.ones((8, ROWS), jnp.float32)
        total = [jnp.zeros((8, ROWS), jnp.float32)] * FIELDS
        d_of = [distances[s, at] for s in range(SLICES + 2)]
        for s in range(SLICES):
            d = d_of[1 + s]
            u = slopes_x[s, at]
            v = slopes_y[s, at] + edges[s, at]
            w = 0.5 * (d_of[2 + s] - d_of[s])
            norm = jnp.maximum(u * u + v * v + w * w, 0.1)
            facing = 0.25 + 0.75 * jnp.abs(w) * lax.rsqrt(norm)
            density = jnp.exp(-2.0 * d * d)
            opacity = 1.0 - jnp.exp(-bricks[3, s, brick] * density)
            weight = transmit * opacity
            shaded = weight * facing
            for f in range(3):
                total[f] = total[f] + shaded * bricks[f, s, brick]
            total[3] = total[3] + weight
            transmit = transmit * (1.0 - opacity)
        for f in range(FIELDS):
            image[chip, f, 8 * part : 8 * part + 8] = total[f]

    def two(i, _):
        for chip in (2 * i, 2 * i + 1):
            for part in range(PIECE // 8):
                tile(chip, part)
        return 0

    lax.fori_loop(0, CHIPS // 2, two, 0)


def given_kernel(core, up, down, kernel_x, kernel_y, distances, slopes_x, slopes_y, bricks, given, edges):
    beside = jnp.concatenate(
        [
            jnp.concatenate([rows[s, 0:1], rows[s, 1:2]], axis=1)
            for s in range(SLICES)
            for rows in (up, down)
        ],
        axis=0,
    )
    beside = halves(product(halves(beside), halves(weights(kernel_x))).T)
    along_y = weights(kernel_y)
    row = iota((2 * SLICES, ROWS), 0)
    for s in range(SLICES):
        wanted = jnp.where(row == 2 * s, -0.5 * along_y[0:1], 0.0) + jnp.where(
            row == 2 * s + 1, 0.5 * along_y[ROWS - 1 : ROWS], 0.0
        )
        edges[s] = product(beside, halves(wanted))
    shade(1 - core[0], distances, slopes_x, slopes_y, edges, bricks, given)


def kept_kernel(core, distances, slopes_x, slopes_y, bricks, edges, kept):
    shade(core[0], distances, slopes_x, slopes_y, edges, bricks, kept)


def over(nearer, farther):
    return nearer + (1.0 - nearer[..., 3:4, :, :]) * farther


def outer_blocks(distance, groups):
    chips = SLICES // 2
    me = lax.axis_index("wide")
    chip, core = me % SLICES // 2, me % 2
    blocks = distance.reshape(chips, 2, COLS, ROWS)
    ends = [pair for k in range(groups) for pair in ((8 * k, 8 * k + 1), (8 * k + 7, 8 * k + 6))]
    shared = lax.ppermute(lax.dynamic_index_in_dim(blocks, 1 - core, 1, keepdims=False), "wide", ends)
    own = lax.dynamic_index_in_dim(blocks, core, 1, keepdims=False)
    first = chip == 0
    given = jnp.where(jnp.where(first, core == 0, core == 1), own, shared)
    before = after = jnp.zeros((COLS, ROWS), jnp.float32)
    for j in (3, 0, 2, 1):
        back = chips - 1 - j
        pairs = []
        for k in range(groups - 1):
            for c in range(2):
                pairs.append((8 * k + 6 + c, 8 * (k + 1) + 2 * j + c))
                pairs.append((8 * (k + 1) + c, 8 * k + 2 * back + c))
        wanted = jnp.where(first, back, j)
        came = lax.ppermute(lax.dynamic_index_in_dim(given, wanted, 0, keepdims=False), "wide", pairs)
        before = jnp.where(chip == j, came, before)
        after = jnp.where(chip == back, came, after)
    return before, after


def local(distance, occupancy, material, colours, absorb, kernel_x, kernel_y):
    slices, col_count, row_count = distance.shape
    wide = lax.axis_size("wide")
    narrow = lax.axis_size("narrow")
    groups = wide // SLICES
    me = lax.axis_index("wide").astype(jnp.int32)
    core = (me & 1).reshape(1)
    members = [[SLICES * k + i for i in range(SLICES)] for k in range(groups)]

    def one(*shape):
        return jax.ShapeDtypeStruct(shape, jnp.float32)

    before, after = outer_blocks(distance, groups)
    message = pl.pallas_call(
        message_kernel,
        out_shape=one(BLOCKS, MESSAGE, ROWS),
        in_specs=[ANY] * 3,
        out_specs=ANY,
        scratch_shapes=[
            pltpu.VMEM((col_count, ROWS), jnp.float32),
            pltpu.VMEM((BLOCKS, MESSAGE - COLS, ROWS), jnp.float32),
            pltpu.VMEM((1, material.shape[2], material.shape[1]), jnp.int32),
            pltpu.VMEM((1, material.shape[2], material.shape[1]), jnp.int32),
            pltpu.SemaphoreType.DMA((2, BLOCKS + 1)),
        ],
        name="message",
    )(distance, jnp.swapaxes(material, 1, 2), jnp.swapaxes(occupancy, 1, 2))
    cells = lax.all_to_all(message, "wide", 0, 0, tiled=True, axis_index_groups=members)
    up = lax.ppermute(cells[:, COLS + 4 : COLS + 6], "narrow", [(i, i + 1) for i in range(narrow - 1)])
    down = lax.ppermute(cells[:, COLS + 2 : COLS + 4], "narrow", [(i + 1, i) for i in range(narrow - 1)])
    step = 4.0 / (slices * wide)
    fields = pl.pallas_call(
        functools.partial(fields_kernel, step),
        out_shape=[
            one(SLICES + 2, COLS, ROWS),
            one(SLICES, COLS, ROWS),
            one(SLICES, COLS, ROWS),
            one(FIELDS, SLICES, COLS // 8, ROWS),
        ],
        in_specs=[VMEM] * 3 + [SMEM] * 2 + [VMEM] * 2,
        out_specs=[VMEM] * 4,
        compiler_params=pltpu.CompilerParams(vmem_limit_bytes=24 * 1024 * 1024),
        cost_estimate=pl.CostEstimate(flops=4 * 10**9, bytes_accessed=6 * 1024 * 1024, transcendentals=0),
        name="fields",
    )(cells, before, after, colours, absorb, kernel_x, kernel_y)
    params = pltpu.CompilerParams(vmem_limit_bytes=24 * 1024 * 1024)
    half = one(CHIPS, FIELDS, PIECE, ROWS)
    given, edges = pl.pallas_call(
        given_kernel,
        out_shape=[half, one(SLICES, COLS, ROWS)],
        in_specs=[SMEM] + [VMEM] * 8,
        out_specs=[VMEM] * 2,
        compiler_params=params,
        name="given",
    )(core, up, down, kernel_x, kernel_y, *fields)
    taken = lax.ppermute(given, "wide", [(i, i ^ 1) for i in range(wide)])
    taken, front = lax.optimization_barrier((taken, jnp.broadcast_to(core == 0, (PIECE, ROWS))))
    kept = pl.pallas_call(
        kept_kernel,
        out_shape=half,
        in_specs=[SMEM] + [VMEM] * 5,
        out_specs=VMEM,
        compiler_params=params,
        cost_estimate=pl.CostEstimate(flops=10**8, bytes_accessed=6 * 1024 * 1024, transcendentals=0),
        name="kept",
    )(core, *fields, edges)
    along_z = [
        [32 * x + 2 * ((z + CHIPS * c) % 16) + c for z in range(16)] for x in range(wide // 32) for c in range(2)
    ]
    parts = lax.all_to_all(
        jnp.concatenate([kept, taken], axis=0), "wide", 0, 0, tiled=True, axis_index_groups=along_z
    )
    parts = parts.reshape(2, 2, 4, FIELDS, PIECE, ROWS)
    halves_z = [over(parts[h, 0], parts[h, 1]) for h in range(2)]
    parts = over(jnp.where(front, halves_z[0], halves_z[1]), jnp.where(front, halves_z[1], halves_z[0]))
    along_x = [[32 * x + i for x in range(4)] for i in range(32)]
    parts = lax.all_to_all(parts, "wide", 0, 0, tiled=True, axis_index_groups=along_x)
    return over(over(parts[0], parts[1]), over(parts[2], parts[3]))


def solution(mesh):
    held = P("wide", None, "narrow")
    return jax.shard_map(
        local,
        mesh=mesh,
        in_specs=(held, held, held, P(), P(), P(), P()),
        out_specs=P(None, "wide", "narrow"),
        check_vma=False,
    )
```

```python
import functools

import jax
import jax.numpy as jnp
from jax import lax
from jax.experimental import pallas as pl
from jax.experimental.pallas import tpu as pltpu
from jax.sharding import PartitionSpec as P

BLOCKS = 8
SLICES = 8
COLS = 256
ROWS = 128
PIECE = 16
CHIPS = 8
MESSAGE = COLS + 16
FIELDS = 4
VMEM = pl.BlockSpec(memory_space=pltpu.VMEM)
SMEM = pl.BlockSpec(memory_space=pltpu.SMEM)
ANY = pl.BlockSpec(memory_space=pl.ANY)


def halves(value):
    high = value.astype(jnp.bfloat16)
    low = (value - high.astype(jnp.float32)).astype(jnp.bfloat16)
    return high, low


def product(a, b, dims=((1,), (0,))):
    a_high, a_low = a
    b_high, b_low = b

    def one(p, q):
        return lax.dot_general(p, q, (dims, ((), ())), preferred_element_type=jnp.float32)

    return one(a_high, b_high) + (one(a_low, b_high) + one(a_high, b_low))


def joined(a, b):
    a_high, a_low = a
    b_high, b_low = b
    return jnp.dot(
        jnp.concatenate([a_high, a_low, a_high], axis=1),
        jnp.concatenate([b_high, b_high, b_low], axis=0),
        preferred_element_type=jnp.float32,
    )


def ones_where(condition):
    return jnp.where(condition, 1.0, 0.0)


def iota(shape, dim):
    return lax.broadcasted_iota(jnp.int32, shape, dim)


def message_kernel(cells, material_in, occupancy_in, message, held, tail, material, occupancy, sems):
    loads, stores = [], []
    brick_loads = [
        pltpu.make_async_copy(material_in, material, sems.at[0, BLOCKS]),
        pltpu.make_async_copy(occupancy_in, occupancy, sems.at[1, BLOCKS]),
    ]
    for load in brick_loads:
        load.start()
    for block in range(BLOCKS):
        part = held.at[block * COLS : (block + 1) * COLS]
        loads.append(pltpu.make_async_copy(cells.at[0, block * COLS : (block + 1) * COLS], part, sems.at[0, block]))
        stores.append(pltpu.make_async_copy(part, message.at[block, :COLS], sems.at[1, block]))
        loads[-1].start()
    ends = jnp.zeros((COLS, ROWS), jnp.float32)
    lane = iota((COLS, ROWS), 1)
    for block in range(BLOCKS):
        loads[block].wait()
        stores[block].start()
        turned = pltpu.roll(held[block * COLS : (block + 1) * COLS], 2 * block + 1, 1)
        ends = jnp.where(lane // 2 == block, turned, ends)
    for load in brick_loads:
        load.wait()
    brick_rows = material.shape[1]
    lane = iota((brick_rows, ROWS), 1)
    row = iota((brick_rows, ROWS), 0)
    kinds = material[0].astype(jnp.float32).T.reshape(BLOCKS, 4, 8, brick_rows)
    masks = occupancy[0].astype(jnp.float32).T.reshape(BLOCKS, 4, 8, brick_rows)
    packed = jnp.zeros((BLOCKS * 8, ROWS), jnp.float32)
    for part in range(4):
        at = 2 * brick_rows * part
        packed += jnp.dot(
            kinds[:, part].reshape(BLOCKS * 8, brick_rows),
            ones_where(lane == row + at),
            preferred_element_type=jnp.float32,
        )
        packed += jnp.dot(
            masks[:, part].reshape(BLOCKS * 8, brick_rows),
            ones_where(lane == row + (at + brick_rows)),
            preferred_element_type=jnp.float32,
        )
    ends = ends.T
    none = jnp.zeros((1, ROWS), jnp.float32)
    for block in range(BLOCKS):
        left, right = block * COLS, (block + 1) * COLS
        tail[block, 0:1] = held[left - 1 : left] if block else none
        tail[block, 1:2] = held[right : right + 1] if block < BLOCKS - 1 else none
        for end in range(2):
            row = 2 * block + 1 - end
            for part in range(2):
                at = 2 + 2 * end + part
                tail[block, at : at + 1] = ends[row : row + 1, part * ROWS : (part + 1) * ROWS]
        tail[block, 6:8] = jnp.zeros((2, ROWS), jnp.float32)
        tail[block, 8:16] = packed[block * 8 : block * 8 + 8]
    stores.append(pltpu.make_async_copy(tail, message.at[:, COLS:MESSAGE], sems.at[0, 0]))
    stores[-1].start()
    for store in stores:
        store.wait()


def weights(kernel):
    size = kernel.shape[0]
    return 0.5 * ones_where(iota((size, size), 0) == iota((size, size), 1)) + kernel[...]


def fields_kernel(
    step, cells, before, after, colours, absorb, kernel_x, kernel_y, distances, slopes_x, slopes_y, bricks
):
    along_x = halves(weights(kernel_x).T)
    along_y = weights(kernel_y)
    none = jnp.zeros((1, ROWS), jnp.float32)
    slope_y = 0.5 * (
        jnp.concatenate([none, along_y[:-1]], axis=0) - jnp.concatenate([along_y[1:], none], axis=0)
    )
    only_y = halves(along_y)
    both_y = halves(jnp.concatenate([along_y, slope_y], axis=1))
    column_ends = jnp.concatenate([cells[s, COLS : COLS + 2] for s in range(SLICES)], axis=0)
    column_ends = product(halves(column_ends), only_y)
    outer = joined(halves(jnp.concatenate([before[...], after[...]], axis=0)), only_y)
    outer = jnp.concatenate([outer[:COLS], outer[COLS:]], axis=1)
    outer = joined(along_x, halves(outer))
    distances[0] = outer[:, :ROWS]
    distances[SLICES + 1] = outer[:, ROWS:]
    for pair in range(SLICES // 2):
        parts = []
        for s in (2 * pair, 2 * pair + 1):
            rows = joined(halves(cells[s, :COLS]), both_y)
            value = rows[:, :ROWS]
            ahead = jnp.concatenate([value[1:], column_ends[2 * s + 1 : 2 * s + 2]], axis=0)
            behind = jnp.concatenate([column_ends[2 * s : 2 * s + 1], value[:-1]], axis=0)
            parts += [value, 0.5 * (ahead - behind), rows[:, ROWS:]]
        mixed = joined(along_x, halves(jnp.concatenate(parts, axis=1)))
        for i, s in enumerate((2 * pair, 2 * pair + 1)):
            at = 3 * i * ROWS
            distances[1 + s] = mixed[:, at : at + ROWS]
            slopes_x[s] = mixed[:, at + ROWS : at + 2 * ROWS]
            slopes_y[s] = mixed[:, at + 2 * ROWS : at + 3 * ROWS]
    codes = cells[:, COLS + 8 : MESSAGE, :].reshape(SLICES * 8, ROWS)
    brick_rows = ROWS // 8
    masks = pltpu.roll(codes, ROWS - brick_rows, 1)
    values = [jnp.zeros_like(codes)] * FIELDS
    for label in range(colours.shape[1]):
        found = codes == float(label)
        for f in range(FIELDS):
            entry = colours[f, label] if f < 3 else absorb[label]
            values[f] = jnp.where(found, entry, values[f])
    values[3] = values[3] * masks * step
    values = jnp.concatenate(values, axis=0)
    source = iota((ROWS, 4 * ROWS), 0)
    target = iota((ROWS, 4 * ROWS), 1)
    spread = ones_where(source == (target // ROWS) * (2 * brick_rows) + (target % ROWS) // 8)
    spread = spread.astype(jnp.bfloat16)
    high, low = halves(values)
    least = (values - high.astype(jnp.float32) - low.astype(jnp.float32)).astype(jnp.bfloat16)
    grown = (
        jnp.dot(least, spread, preferred_element_type=jnp.float32)
        + jnp.dot(low, spread, preferred_element_type=jnp.float32)
        + jnp.dot(high, spread, preferred_element_type=jnp.float32)
    )
    for f in range(FIELDS):
        for s in range(SLICES):
            for part in range(4):
                bricks[f, s, 8 * part : 8 * part + 8] = grown[
                    (f * SLICES + s) * 8 : (f * SLICES + s) * 8 + 8, part * ROWS : (part + 1) * ROWS
                ]


def shade(core, distances, slopes_x, slopes_y, edges, bricks, image):
    def tile(chip, part):
        row = (2 * chip + core) * (PIECE // 8) + part
        at = pl.ds(pl.multiple_of(row * 8, 8), 8)
        brick = pl.ds(row, 1)
        transmit = jnp.ones((8, ROWS), jnp.float32)
        total = [jnp.zeros((8, ROWS), jnp.float32)] * FIELDS
        d_of = [distances[s, at] for s in range(SLICES + 2)]
        for s in range(SLICES):
            d = d_of[1 + s]
            u = slopes_x[s, at]
            v = slopes_y[s, at] + edges[s, at]
            w = 0.5 * (d_of[2 + s] - d_of[s])
            norm = jnp.maximum(u * u + v * v + w * w, 0.1)
            facing = 0.25 + 0.75 * jnp.abs(w) * lax.rsqrt(norm)
            density = jnp.exp(-2.0 * d * d)
            opacity = 1.0 - jnp.exp(-bricks[3, s, brick] * density)
            weight = transmit * opacity
            shaded = weight * facing
            for f in range(3):
                total[f] = total[f] + shaded * bricks[f, s, brick]
            total[3] = total[3] + weight
            transmit = transmit * (1.0 - opacity)
        for f in range(FIELDS):
            image[chip, f, 8 * part : 8 * part + 8] = total[f]

    def two(i, _):
        for chip in (2 * i, 2 * i + 1):
            for part in range(PIECE // 8):
                tile(chip, part)
        return 0

    lax.fori_loop(0, CHIPS // 2, two, 0)


def given_kernel(core, up, down, kernel_x, kernel_y, distances, slopes_x, slopes_y, bricks, given, edges):
    beside = jnp.concatenate(
        [
            jnp.concatenate([rows[s, 0:1], rows[s, 1:2]], axis=1)
            for s in range(SLICES)
            for rows in (up, down)
        ],
        axis=0,
    )
    beside = halves(product(halves(beside), halves(weights(kernel_x))).T)
    along_y = weights(kernel_y)
    row = iota((2 * SLICES, ROWS), 0)
    for s in range(SLICES):
        wanted = jnp.where(row == 2 * s, -0.5 * along_y[0:1], 0.0) + jnp.where(
            row == 2 * s + 1, 0.5 * along_y[ROWS - 1 : ROWS], 0.0
        )
        edges[s] = product(beside, halves(wanted))
    shade(1 - core[0], distances, slopes_x, slopes_y, edges, bricks, given)


def kept_kernel(core, distances, slopes_x, slopes_y, bricks, edges, kept):
    shade(core[0], distances, slopes_x, slopes_y, edges, bricks, kept)


def over(nearer, farther):
    return nearer + (1.0 - nearer[..., 3:4, :, :]) * farther


def outer_blocks(distance, groups):
    chips = SLICES // 2
    me = lax.axis_index("wide")
    chip, core = me % SLICES // 2, me % 2
    blocks = distance.reshape(chips, 2, COLS, ROWS)
    ends = [pair for k in range(groups) for pair in ((8 * k, 8 * k + 1), (8 * k + 7, 8 * k + 6))]
    shared = lax.ppermute(lax.dynamic_index_in_dim(blocks, 1 - core, 1, keepdims=False), "wide", ends)
    own = lax.dynamic_index_in_dim(blocks, core, 1, keepdims=False)
    first = chip == 0
    given = jnp.where(jnp.where(first, core == 0, core == 1), own, shared)
    before = after = jnp.zeros((COLS, ROWS), jnp.float32)
    for j in range(chips):
        back = chips - 1 - j
        pairs = []
        for k in range(groups - 1):
            for c in range(2):
                pairs.append((8 * k + 6 + c, 8 * (k + 1) + 2 * j + c))
                pairs.append((8 * (k + 1) + c, 8 * k + 2 * back + c))
        wanted = jnp.where(first, back, j)
        came = lax.ppermute(lax.dynamic_index_in_dim(given, wanted, 0, keepdims=False), "wide", pairs)
        before = jnp.where(chip == j, came, before)
        after = jnp.where(chip == back, came, after)
    return before, after


def local(distance, occupancy, material, colours, absorb, kernel_x, kernel_y):
    slices, col_count, row_count = distance.shape
    wide = lax.axis_size("wide")
    narrow = lax.axis_size("narrow")
    groups = wide // SLICES
    me = lax.axis_index("wide").astype(jnp.int32)
    core = (me & 1).reshape(1)
    members = [[SLICES * k + i for i in range(SLICES)] for k in range(groups)]

    def one(*shape):
        return jax.ShapeDtypeStruct(shape, jnp.float32)

    before, after = outer_blocks(distance, groups)
    message = pl.pallas_call(
        message_kernel,
        out_shape=one(BLOCKS, MESSAGE, ROWS),
        in_specs=[ANY] * 3,
        out_specs=ANY,
        scratch_shapes=[
            pltpu.VMEM((col_count, ROWS), jnp.float32),
            pltpu.VMEM((BLOCKS, MESSAGE - COLS, ROWS), jnp.float32),
            pltpu.VMEM((1, material.shape[2], material.shape[1]), jnp.int32),
            pltpu.VMEM((1, material.shape[2], material.shape[1]), jnp.int32),
            pltpu.SemaphoreType.DMA((2, BLOCKS + 1)),
        ],
        name="message",
    )(distance, jnp.swapaxes(material, 1, 2), jnp.swapaxes(occupancy, 1, 2))
    cells = lax.all_to_all(message, "wide", 0, 0, tiled=True, axis_index_groups=members)
    up = lax.ppermute(cells[:, COLS + 4 : COLS + 6], "narrow", [(i, i + 1) for i in range(narrow - 1)])
    down = lax.ppermute(cells[:, COLS + 2 : COLS + 4], "narrow", [(i + 1, i) for i in range(narrow - 1)])
    step = 4.0 / (slices * wide)
    fields = pl.pallas_call(
        functools.partial(fields_kernel, step),
        out_shape=[
            one(SLICES + 2, COLS, ROWS),
            one(SLICES, COLS, ROWS),
            one(SLICES, COLS, ROWS),
            one(FIELDS, SLICES, COLS // 8, ROWS),
        ],
        in_specs=[VMEM] * 3 + [SMEM] * 2 + [VMEM] * 2,
        out_specs=[VMEM] * 4,
        compiler_params=pltpu.CompilerParams(vmem_limit_bytes=24 * 1024 * 1024),
        cost_estimate=pl.CostEstimate(flops=4 * 10**9, bytes_accessed=6 * 1024 * 1024, transcendentals=0),
        name="fields",
    )(cells, before, after, colours, absorb, kernel_x, kernel_y)
    params = pltpu.CompilerParams(vmem_limit_bytes=24 * 1024 * 1024)
    half = one(CHIPS, FIELDS, PIECE, ROWS)
    given, edges = pl.pallas_call(
        given_kernel,
        out_shape=[half, one(SLICES, COLS, ROWS)],
        in_specs=[SMEM] + [VMEM] * 8,
        out_specs=[VMEM] * 2,
        compiler_params=params,
        name="given",
    )(core, up, down, kernel_x, kernel_y, *fields)
    taken = lax.ppermute(given, "wide", [(i, i ^ 1) for i in range(wide)])
    taken, front = lax.optimization_barrier((taken, jnp.broadcast_to(core == 0, (PIECE, ROWS))))
    kept = pl.pallas_call(
        kept_kernel,
        out_shape=half,
        in_specs=[SMEM] + [VMEM] * 5,
        out_specs=VMEM,
        compiler_params=params,
        cost_estimate=pl.CostEstimate(flops=10**8, bytes_accessed=6 * 1024 * 1024, transcendentals=0),
        name="kept",
    )(core, *fields, edges)
    along_z = [
        [32 * x + 2 * ((z + CHIPS * c) % 16) + c for z in range(16)] for x in range(wide // 32) for c in range(2)
    ]
    parts = lax.all_to_all(
        jnp.concatenate([kept, taken], axis=0), "wide", 0, 0, tiled=True, axis_index_groups=along_z
    )
    parts = parts.reshape(2, 2, 4, FIELDS, PIECE, ROWS)
    halves_z = [over(parts[h, 0], parts[h, 1]) for h in range(2)]
    parts = over(jnp.where(front, halves_z[0], halves_z[1]), jnp.where(front, halves_z[1], halves_z[0]))
    along_x = [[32 * x + i for x in range(4)] for i in range(32)]
    parts = lax.all_to_all(parts, "wide", 0, 0, tiled=True, axis_index_groups=along_x)
    return over(over(parts[0], parts[1]), over(parts[2], parts[3]))


def solution(mesh):
    held = P("wide", None, "narrow")
    return jax.shard_map(
        local,
        mesh=mesh,
        in_specs=(held, held, held, P(), P(), P(), P()),
        out_specs=P(None, "wide", "narrow"),
        check_vma=False,
    )
```
